32 devices in a mesh: ctx: 2 (over x), row: 2 (over core), exp: 8 (over z, y).
Axes of the slice: x: 2, y: 2, z: 4, core: 2. Of those that a mesh axis runs over, the one named last changes fastest.
Arguments:
- queries: bfloat16 [64, 128, 576], P(('row', 'exp')), may hold values from -10 to 10
- latent_cache: bfloat16 [64, 8192, 576], P(('row', 'exp'), 'ctx'), may hold values from -6 to 6
- lengths: int32 [64], P(('row', 'exp')), may hold values from 512 to 8192, as said below
- w_value: bfloat16 [128, 512, 128], P(('ctx', 'exp')), may hold values from -0.25 to 0.25
- w_out: bfloat16 [16384, 7168], P(('ctx', 'exp')), may hold values from -0.0625 to 0.0625
- stream: bfloat16 [64, 7168], P(('row', 'exp'), 'ctx'), may hold values from -6 to 6
- norm_gain: float32 [7168], P('ctx'), may hold values from 0.1 to 1.9
- expert_ids: int32 [64, 8], P(('row', 'exp')), may hold values from 0 to 15, all different within a row; in each aligned block of 4 rows (0 to 3, 4 to 7, ...) at most 2 rows name the same one
- gate_weights: float32 [64, 8], P(('row', 'exp')), may hold values from 0.1 to 0.6
- w_gate: bfloat16 [16, 7168, 1024], P(('row', 'exp'), 'ctx'), may hold values from -0.0625 to 0.0625
- w_up: bfloat16 [16, 7168, 1024], P(('row', 'exp'), 'ctx'), may hold values from -0.0625 to 0.0625
- w_down: bfloat16 [16, 1024, 7168], P(('row', 'exp'), None, 'ctx'), may hold values from -0.1875 to 0.1875
Outputs:
- layer_out: bfloat16 [64, 7168], P(('row', 'exp'), 'ctx')
The draws below stay inside these ranges and needn't reach their ends.
Inputs may be any that keep to these rules, and one draw needn't show every extreme that they name: `lengths`: some row has 8192 live positions and some row 512. `expert_ids`: each row names 8 different experts; among the 4 rows of one device no expert is named by more than 2 rows.
All inputs are finite; a program needn't handle non-finite values.
Results may differ from the reference program's by a relative error of at most 0.012.
Values may be sent and summed in bfloat16 or wider, within the bound.
A program may use at most 128 MiB of HBM per device.

```python
import math
import jax
import jax.numpy as jnp
import numpy as np
from jax import lax

D = 7168
HEADS = 128
LAT = 512
ROPE = 64
QK_HEAD = 192
V_HEAD = 128
TOP = 8
FFE = 1024
ROW_GRP = 4
LENGTH = 8192
BLOCK = 4096
ROWS = 64
EXPERTS = 16
CAP = 2
N_CTX = 2


def draw_latent_cache(key, part):
    key = jax.random.fold_in(key, 7)
    shape = (ROWS, LENGTH, LAT + ROPE)
    base = jnp.clip(jax.random.normal(key, shape, jnp.float32), -6.0, 6.0)
    return base.astype(jnp.bfloat16)


def draw_queries(key, part):
    key = jax.random.fold_in(key, 9)
    shape = (ROWS, HEADS, LAT + ROPE)
    base = jnp.clip(jax.random.normal(key, shape, jnp.float32), -6.0, 6.0)
    return base.astype(jnp.bfloat16)


def draw_lengths(key, part):
    key = jax.random.fold_in(key, 5)
    drawn = jax.random.randint(key, (ROWS,), LENGTH // 16, LENGTH + 1)
    row_numbers = jnp.arange(ROWS)
    drawn = jnp.where(row_numbers == 0, LENGTH, drawn)
    drawn = jnp.where(row_numbers == 1, LENGTH // 16, drawn)
    return drawn.astype(jnp.int32)


def raised(entries, rng, source, target, parts, factor):
    def block_of(axis_at):
        return (jnp.arange(entries.shape[axis_at]) // (entries.shape[axis_at] // parts)).reshape((-1,) + (1,) * (entries.ndim - 1 - axis_at))

    one_side = jax.random.permutation(rng, parts)[block_of(target)]
    other_side = (block_of(target) + parts // 2) % parts
    return jnp.where((block_of(source) == one_side) | (block_of(source) == other_side), factor * entries, entries)


def shard_levels(rng, dims, shards, low, high):
    factor_of, own = 1.0, jax.random.fold_in(rng, 6)
    for dim, blocks in shards:
        draws = jnp.exp(jax.random.uniform(jax.random.fold_in(own, dim), (blocks,), jnp.float32, low / len(shards), high / len(shards)))
        factor_of = factor_of * jnp.repeat(draws, dims[dim] // blocks).reshape([-1 if axis == dim else 1 for axis in range(len(dims))])
    return factor_of


def routed_block(own_key, own, number, rows, count, top, bound, lean):
    ranking = jax.random.permutation(own_key, count)
    packed, usual = shares(count, rows * top, bound, lean, True), shares(count, rows * top, bound, lean, False)
    places = jnp.arange(count)

    def named(sizes, offset_by):
        used = int((sizes > 0).sum())
        fixed = max(1, used // 4)
        passed = fixed + (places - fixed + offset_by * (used - fixed)) % max(1, count - fixed)
        return jnp.zeros((count,), jnp.int32).at[ranking[jnp.where(places < fixed, places, passed)]].set(jnp.asarray(sizes, jnp.int32))

    sizes = jnp.where(number % 4 == 0, named(packed, number // 4), named(usual, number - number // 4 - 1))
    mixed = jax.random.permutation(jax.random.fold_in(own, 3), count)
    giver, sink = mixed[0:count // 2 * 2:2], mixed[1:count // 2 * 2:2]
    slack = jnp.minimum(sizes[giver] - 1, bound - sizes[sink]) // 2
    slack = jnp.where((giver == ranking[0]) | (sink == ranking[0]) | (sizes[sink] == 0), 0, jnp.maximum(slack, 0))
    passed = jax.random.randint(jax.random.fold_in(own, 4), (count // 2,), 0, 1 << 20) % (slack + 1)
    sizes = sizes.at[giver].add(-passed).at[sink].add(passed)
    labels = jnp.searchsorted(jnp.cumsum(sizes), jnp.arange(rows * top), side="right").astype(jnp.int32)
    grid = labels.reshape(top, rows).T
    grid = grid[jax.random.permutation(jax.random.fold_in(own, 1), rows)]
    offset_by = jax.random.randint(jax.random.fold_in(own, 2), (rows, 1), 0, top)
    return jnp.take_along_axis(grid, (jnp.arange(top)[None, :] + offset_by) % top, axis=1)


def shares(amount, total, most, lean, full):
    portions = [(1 << 20) // math.isqrt(grade ** lean) + 1 for grade in range(1, amount + 1)]
    largest = most if full else min(most, max(-(-total // amount), total * portions[0] // sum(portions)))
    least = 1 if total - largest >= amount - 1 else 0
    counts, spare = [largest] + [least] * (amount - 1), total - largest - least * (amount - 1)
    while spare > 0:
        movable = [i for i in range(1, amount) if counts[i] < largest] or [i for i in range(1, amount) if counts[i] < most]
        mass, left = sum([portions[i] for i in movable]), spare
        for i in movable:
            extra = min(most - counts[i], max(1, left * portions[i] // mass), spare)
            counts[i] = counts[i] + extra
            spare = spare - extra
    return np.array(counts)


def bell_draw(own_key, shape, scale, limit, pieces=(), kind=jnp.bfloat16):
    gain = shard_levels(own_key, shape, pieces, -0.22, 0.18) if pieces else 1.0
    values = jax.random.normal(own_key, shape, jnp.float32) * scale * gain
    return jnp.minimum(jnp.maximum(values, -limit), limit).astype(kind)


def heavy_noise(stream_key, shape, scale, most, shards, heavy, kind=jnp.bfloat16):
    entries = scale * jax.random.normal(stream_key, shape, jnp.float32)
    if shards:
        entries = entries * shard_levels(stream_key, shape, shards, -0.22, 0.18)
    return jnp.clip(raised(entries, jax.random.fold_in(stream_key, 3), *heavy), -most, most).astype(kind)


def setup_inputs(seed: int = 0) -> dict:
    splits = jax.random.split(jax.random.key(seed), 13)
    queries = draw_queries(jax.random.fold_in(splits[12], 71), 0)
    latent_cache = draw_latent_cache(jax.random.fold_in(splits[12], 71), 0)
    lengths = draw_lengths(jax.random.fold_in(splits[12], 71), 0)
    w_value = bell_draw(splits[3], (HEADS, LAT, V_HEAD), LAT ** -0.5, 0.25, ((0, 16),))
    w_out = heavy_noise(splits[4], (HEADS * V_HEAD, D), (HEADS * V_HEAD) ** -0.5, 0.0625, ((0, 16),), (0, 1, 16, 2.0))
    stream = bell_draw(splits[5], (ROWS, D), 1.0, 6.0, ((0, 16), (1, 2)))
    norm_gain = jnp.clip(1.0 + 0.18 * jax.random.normal(splits[6], (D,), jnp.float32), 0.1, 1.9)
    expert_ids_keys = jax.random.split(jax.random.fold_in(splits[7], 1), ROWS // ROW_GRP)
    expert_ids_turns = jax.random.permutation(jax.random.fold_in(splits[7], 3), ROWS // ROW_GRP)
    expert_ids = jax.vmap(lambda own, number: routed_block(jax.random.fold_in(splits[7], 2), own, number, ROW_GRP, EXPERTS, TOP, CAP, 2))(expert_ids_keys, expert_ids_turns).reshape((ROWS, TOP))
    gate_weights = jnp.clip(0.1 + 0.5 * jax.random.uniform(splits[8], (ROWS, TOP), jnp.float32) ** shard_levels(splits[8], (ROWS, TOP), ((0, 16),), -0.2, 0.2), 0.1, 0.6)
    w_gate = bell_draw(splits[9], (EXPERTS, D, FFE), D ** -0.5, 0.0625, ((0, 16), (1, 2)))
    w_up = bell_draw(splits[10], (EXPERTS, D, FFE), D ** -0.5, 0.0625, ((0, 16), (1, 2)))
    w_down = bell_draw(splits[11], (EXPERTS, FFE, D), FFE ** -0.5, 0.1875, ((0, 16), (2, 2)))
    return dict(queries=queries, latent_cache=latent_cache, lengths=lengths, w_value=w_value, w_out=w_out, stream=stream, norm_gain=norm_gain, expert_ids=expert_ids, gate_weights=gate_weights, w_gate=w_gate, w_up=w_up, w_down=w_down)


epsilon = 1e-06

def attend_row(inputs):
    query_row, cache_row, length = inputs
    scores = jnp.dot(query_row, cache_row.T, preferred_element_type=jnp.float32) * QK_HEAD ** (-0.5)
    scores = scores.reshape(HEADS, N_CTX, BLOCK)
    position = jnp.arange(LENGTH, dtype=jnp.int32).reshape(N_CTX, BLOCK)
    live = (position < length)[None]
    block_max = lax.optimization_barrier(jnp.max(jnp.where(live, scores, -jnp.inf), axis=2))
    shift_by = jnp.where(jnp.isfinite(block_max), block_max, 0.0)
    weights = jnp.where(live, jnp.exp(scores - shift_by[:, :, None]), 0.0)
    totals = lax.optimization_barrier(jnp.sum(weights, axis=2))
    weights_low = lax.optimization_barrier(weights.astype(jnp.bfloat16))
    latent_part = cache_row[:, :LAT].reshape(N_CTX, BLOCK, LAT)
    block_out = jnp.einsum('hcs,csl->hcl', weights_low.astype(jnp.float32), latent_part.astype(jnp.float32))
    top_value = lax.optimization_barrier(jnp.max(block_max, axis=1))
    factor = jnp.exp(block_max - top_value[:, None])
    numer = lax.optimization_barrier(jnp.sum(factor[:, :, None] * block_out, axis=1))
    denom = lax.optimization_barrier(jnp.sum(factor * totals, axis=1))
    return (numer / denom[:, None]).astype(jnp.bfloat16)

def reference(queries, latent_cache, lengths, w_value, w_out, stream, norm_gain, expert_ids, gate_weights, w_gate, w_up, w_down):
    attended = lax.map(attend_row, (queries, latent_cache, lengths))
    attended = lax.optimization_barrier(attended)
    values = jnp.einsum('bhl,hlv->bhv', attended.astype(jnp.float32), w_value.astype(jnp.float32))
    values = values.astype(jnp.bfloat16).reshape(ROWS, HEADS * V_HEAD)
    attn_out = jnp.dot(values, w_out, preferred_element_type=jnp.float32)
    hidden = lax.optimization_barrier((stream.astype(jnp.float32) + attn_out).astype(jnp.bfloat16))
    hidden_wide = hidden.astype(jnp.float32)
    inverse = lax.rsqrt(lax.optimization_barrier(jnp.sum(hidden_wide * hidden_wide, axis=1)) / D + epsilon)
    scaled = (hidden_wide * norm_gain[None, :]).astype(jnp.bfloat16)
    flat_ids = expert_ids.reshape(-1).astype(jnp.int32)
    row_index = jnp.arange(ROWS * TOP, dtype=jnp.int32) // TOP

    def expert_pair(inputs):
        row_at, expert_at = inputs
        vector = scaled[row_at]
        factor = inverse[row_at]
        gate_pre = factor * jnp.dot(vector, w_gate[expert_at], preferred_element_type=jnp.float32)
        up_pre = factor * jnp.dot(vector, w_up[expert_at], preferred_element_type=jnp.float32)
        active = (jax.nn.silu(gate_pre) * up_pre).astype(jnp.bfloat16)
        return jnp.dot(active, w_down[expert_at], preferred_element_type=jnp.float32).astype(jnp.bfloat16)
    produced = lax.map(expert_pair, (row_index, flat_ids))
    produced = lax.optimization_barrier(produced).reshape(ROWS, TOP, D)
    mixture = lax.optimization_barrier(jnp.sum(gate_weights[:, :, None] * produced.astype(jnp.float32), axis=1))
    return (hidden_wide + mixture).astype(jnp.bfloat16)
```

```python
import math

import jax
import jax.numpy as jnp
from jax import lax
from jax.experimental import pallas as pl
from jax.experimental.pallas import tpu as pltpu
from jax.sharding import PartitionSpec as P

D = 7168
QK_HEAD = 192


epsilon = 1e-06


def merge_blocks(outputs, maxima, totals):
    top_value = jnp.max(maxima, axis=0)
    factor = jnp.exp(maxima - top_value[None])
    numer = jnp.sum(factor[..., None] * outputs, axis=0)
    denom = jnp.sum(factor * totals, axis=0)
    return (numer / denom[..., None]).astype(jnp.bfloat16)


def on_device(
    queries,
    latent_cache,
    lengths,
    w_value,
    w_out,
    stream,
    norm_gain,
    expert_ids,
    gate_weights,
    w_gate,
    w_up,
    w_down,
):
    n_ctx = lax.axis_size("ctx")
    n_row = lax.axis_size("row")
    n_exp = lax.axis_size("exp")
    groups = queries.shape[0]
    block = latent_cache.shape[1]
    per_dev = w_value.shape[0]
    latent = w_value.shape[1]
    scores = jnp.einsum(
        "bhw,btw->bht", queries, latent_cache, preferred_element_type=jnp.float32
    ) * QK_HEAD ** (-0.5)
    position = lax.axis_index("ctx") * block + jnp.arange(block, dtype=jnp.int32)
    live = (position[None, :] < lengths[:, None])[:, None, :]
    block_max = jnp.max(jnp.where(live, scores, -jnp.inf), axis=2)
    shift_by = jnp.where(jnp.isfinite(block_max), block_max, 0.0)
    weights = jnp.where(live, jnp.exp(scores - shift_by[..., None]), 0.0)
    totals = jnp.sum(weights, axis=2)
    latent_out = jnp.einsum(
        "bht,btl->bhl",
        weights.astype(jnp.bfloat16),
        latent_cache[:, :, :latent],
        preferred_element_type=jnp.float32,
    )
    outputs, maxima, sums = (
        lax.all_to_all(
            latent_out.reshape(1, groups, n_ctx * n_exp, per_dev, latent),
            ("ctx", "exp"),
            split_axis=2,
            concat_axis=0,
            tiled=True,
        ),
        lax.all_to_all(
            block_max.reshape(1, groups, n_ctx * n_exp, per_dev),
            ("ctx", "exp"),
            split_axis=2,
            concat_axis=0,
            tiled=True,
        ),
        lax.all_to_all(
            totals.reshape(1, groups, n_ctx * n_exp, per_dev),
            ("ctx", "exp"),
            split_axis=2,
            concat_axis=0,
            tiled=True,
        ),
    )
    gathered_rows = n_exp * groups
    attended = merge_blocks(
        outputs.reshape(n_ctx, gathered_rows, per_dev, latent),
        maxima.reshape(n_ctx, gathered_rows, per_dev),
        sums.reshape(n_ctx, gathered_rows, per_dev),
    )
    values = jnp.einsum("nhl,hlv->nhv", attended, w_value, preferred_element_type=jnp.float32)
    values = values.astype(jnp.bfloat16).reshape(gathered_rows, -1)
    split_out = w_out.reshape(w_out.shape[0], n_ctx, -1)
    term_rows = jnp.einsum(
        "nk,kcd->cnd", values, split_out, preferred_element_type=jnp.float32
    ).reshape(n_ctx * gathered_rows, -1)
    attn_out = lax.psum_scatter(term_rows, ("ctx", "exp"), scatter_dimension=0, tiled=True)
    hidden = lax.optimization_barrier((stream.astype(jnp.float32) + attn_out).astype(jnp.bfloat16))
    experts = n_row * n_exp
    picks = expert_ids.shape[1]
    capacity = max(2, (groups * picks + experts - 1) // experts)
    expert_range = jnp.arange(experts, dtype=jnp.int32)
    onehot = expert_ids[:, :, None] == expert_range[None, None, :]
    named = jnp.sum(onehot.astype(jnp.int32), axis=1)
    slot_of = jnp.cumsum(named, axis=0) - named
    slot_match = slot_of[:, :, None] == jnp.arange(capacity, dtype=jnp.int32)[None, None, :]
    placed = (named[:, :, None] == 1) & slot_match
    outgoing = jnp.einsum(
        "bxs,bd->xsd", placed.astype(jnp.bfloat16), hidden, preferred_element_type=jnp.float32
    ).astype(jnp.bfloat16)
    width_dev = outgoing.shape[2]
    arrived = lax.all_to_all(outgoing, ("row", "exp"), split_axis=0, concat_axis=0, tiled=True)
    arrived = arrived.reshape(experts * capacity, width_dev)
    arrived_wide = arrived.astype(jnp.float32)
    sumsq = jnp.sum(arrived_wide * arrived_wide, axis=1)
    scaled = (arrived_wide * norm_gain[None, :]).astype(jnp.bfloat16)
    gate_part = jnp.dot(scaled, w_gate[0], preferred_element_type=jnp.float32)
    up_part = jnp.dot(scaled, w_up[0], preferred_element_type=jnp.float32)
    gate_part, up_part, sumsq = lax.psum((gate_part, up_part, sumsq), "ctx")
    inverse = lax.rsqrt(sumsq / D + epsilon)[:, None]
    active = (jax.nn.silu(inverse * gate_part) * (inverse * up_part)).astype(jnp.bfloat16)
    produced = jnp.dot(active, w_down[0], preferred_element_type=jnp.float32).astype(jnp.bfloat16)
    returned = lax.all_to_all(
        produced.reshape(experts, capacity, width_dev),
        ("row", "exp"),
        split_axis=0,
        concat_axis=0,
        tiled=True,
    )
    weighted = jnp.sum(gate_weights[:, :, None] * onehot.astype(jnp.float32), axis=1)
    combine = weighted[:, :, None] * slot_match.astype(jnp.float32)
    mixture = jnp.einsum(
        "bxs,xsd->bd", combine, returned.astype(jnp.float32), precision=lax.Precision.HIGHEST
    )
    return (hidden.astype(jnp.float32) + mixture).astype(jnp.bfloat16)


F32 = jnp.float32
BF16 = jnp.bfloat16
MESH = pl.DeviceIdType.MESH
DEAD = -1e30
FLOOR = -1e29
RATE = QK_HEAD ** (-0.5) * math.log2(math.e)


def iota(shape, dim):
    return lax.broadcasted_iota(jnp.int32, shape, dim)


def mm(a, b):
    return jnp.dot(a, b, preferred_element_type=F32)


def onehot(cond):
    return jnp.where(cond, 1.0, 0.0).astype(BF16)


def routing(expert, ids, gates, rows, picks):
    weights, slots = [], []
    before = jnp.zeros(expert.shape, jnp.int32)
    for b in range(rows):
        weight = jnp.zeros(expert.shape, F32)
        for k in range(picks):
            weight = jnp.where(expert == ids[b, k], gates[b, k], weight)
        weights.append(weight)
        slots.append(before)
        before = before + jnp.where(weight > 0.0, 1, 0)
    return weights, slots


def layer_kernel(
    queries, cache_hbm, lengths, wv_hbm, wo_hbm, stream, gain, ids, gates, wg_hbm, wu_hbm, wd_hbm,
    out,
    cache, wv, wo, wg, wu, wd,
    scores, msg, xr, atf, ats, ar, vals, osend, oown, orecv, packed, rsend, rrecv, hid4, blocks,
    tsend, trecv, xsel, gusend, gurecv, sqsend, sqrecv, made, psend, precv, combine,
    cache_sem, w_sem, x_ss, x_rs, a_ss, a_rs, o_ss, o_rs, r_ss, r_rs, g_ss, g_rs, t_ss, t_rs,
    u_ss, u_rs, p_ss, p_rs,
):
    rows, heads, _ = queries.shape
    block = cache_hbm.shape[1]
    latent = wv_hbm.shape[1]
    n_exp = lax.axis_size("exp")
    devs = lax.axis_size("row") * n_exp
    picks = ids.shape[1]
    per_dev = wv_hbm.shape[0]
    width = stream.shape[1]
    part = width // 4
    c, r, e = lax.axis_index("ctx"), lax.axis_index("row"), lax.axis_index("exp")
    g = r * n_exp + e
    z, y = e // 2, lax.rem(e, 2)
    half_heads = heads // 2

    def remote(src, dst, ss, rs, ctx=None, row=None, exp=None):
        where = {
            "ctx": c if ctx is None else ctx,
            "row": r if row is None else row,
            "exp": e if exp is None else exp,
        }
        return pltpu.make_async_remote_copy(
            src_ref=src, dst_ref=dst, send_sem=ss, recv_sem=rs, device_id=where, device_id_type=MESH
        )

    def each(low, high, body):
        def step(i, carry):
            body(i)
            return carry

        lax.fori_loop(low, high, step, 0)

    def cache_copy(b):
        slot = lax.rem(b, 2)
        return pltpu.make_async_copy(cache_hbm.at[b], cache.at[slot], cache_sem.at[slot])

    def half_of(i):
        side = (1 - c) if i == 0 else c
        return wo_hbm.at[:, pl.ds(pl.multiple_of(side * width, 128), width)]

    weight_copies = [
        pltpu.make_async_copy(wv_hbm, wv, w_sem.at[0]),
        pltpu.make_async_copy(half_of(0), wo.at[0], w_sem.at[1]),
        pltpu.make_async_copy(half_of(1), wo.at[1], w_sem.at[2]),
        pltpu.make_async_copy(wg_hbm.at[0], wg, w_sem.at[3]),
        pltpu.make_async_copy(wu_hbm.at[0], wu, w_sem.at[4]),
        pltpu.make_async_copy(wd_hbm.at[0], wd, w_sem.at[5]),
    ]

    cache_copy(0).start()
    cache_copy(1).start()

    barrier = pltpu.get_barrier_semaphore()
    pl.semaphore_signal(
        barrier, inc=1, device_id={"ctx": 1 - c, "row": r, "exp": e}, device_id_type=MESH
    )

    def greet(d):
        to = lax.rem(g + d, devs)
        pl.semaphore_signal(
            barrier, inc=1, device_id={"ctx": c, "row": to // n_exp, "exp": lax.rem(to, n_exp)},
            device_id_type=MESH,
        )

    each(1, devs, greet)

    shape = (devs, 8, 128)
    expert, sub, lane = iota(shape, 0), iota(shape, 1), iota(shape, 2)
    weights, slots = routing(expert, ids, gates, rows, picks)
    tile = jnp.zeros(shape, F32)
    for b in range(rows):
        here = ((lane & 3) == b) & (sub == 2 * lax.rem(g, 4) + slots[b])
        tile = jnp.where(here, weights[b], tile)
    tsend[...] = tile
    trecv[g] = tsend[g]

    shape = (32, devs * 16)
    line, col = iota(shape, 0), iota(shape, 1)
    weights, slots = routing(col >> 4, ids, gates, rows, picks)
    comb = jnp.zeros(shape, F32)
    for b in range(rows):
        here = ((line & 3) == b) & ((line >> 2) == ((col & 15) >> 1)) & ((col & 1) == slots[b])
        comb = jnp.where(here, weights[b], comb)
    high = comb.astype(BF16)
    combine[0:32, :] = high
    combine[32:64, :] = (comb - high.astype(F32)).astype(BF16)

    pl.semaphore_wait(barrier, devs)

    def tile_copy(d, back=False):
        to = lax.rem(g + d, devs)
        return remote(
            tsend.at[to], trecv.at[to if back else g], t_ss.at[to], t_rs.at[to if back else g],
            row=to // n_exp, exp=lax.rem(to, n_exp),
        )

    each(1, devs, lambda d: tile_copy(d).start())

    def swap(b):
        return remote(msg.at[b, 1 - c], xr.at[b], x_ss.at[b], x_rs.at[b], ctx=1 - c)

    def att_copy(pair, d, back=False):
        to = lax.rem(e + d, n_exp)
        return remote(
            ats.at[pair, to], ar.at[to if back else e, pair],
            a_ss.at[pair, to], a_rs.at[pair, to if back else e], exp=to,
        )

    def attend(b):
        slot = lax.rem(b, 2)
        cache_copy(b).wait()
        query = queries[b]
        live = lengths[b] - c * block
        step = 1024
        tops = []
        for t in range(block // step):
            span = slice(t * step, (t + 1) * step)
            s = lax.dot_general(
                query, cache[slot, span, :], (((1,), (1,)), ((), ())), preferred_element_type=F32
            )
            s = jnp.where(iota(s.shape, 1) + t * step < live, s, DEAD)
            scores[:, span] = s
            tops.append(jnp.max(s, axis=1, keepdims=True))
        top = tops[0]
        for other in tops[1:]:
            top = jnp.maximum(top, other)
        top = jnp.maximum(top, FLOOR).astype(BF16).astype(F32)
        total = jnp.zeros_like(top)
        acc = jnp.zeros((heads, latent), F32)
        for t in range(block // step):
            span = slice(t * step, (t + 1) * step)
            p = jnp.exp2((scores[:, span] - top) * RATE)
            total += jnp.sum(p, axis=1, keepdims=True)
            acc += mm(p.astype(BF16), cache[slot, span, 0:latent])
        lane = iota((heads, 128), 1)
        rest = total - total.astype(BF16).astype(F32)
        aux = jnp.where(lane == 0, top, jnp.where(lane == 1, total, jnp.where(lane == 2, rest, 0.0)))
        acc, aux = acc.astype(BF16), aux.astype(BF16)
        for side in range(2):
            mine = slice(side * half_heads, (side + 1) * half_heads)
            msg[b, side, :, 0:latent] = acc[mine]
            msg[b, side, :, latent : latent + 128] = aux[mine]
        swap(b).start()

    def merge(b, pair, last):
        swap(b).wait_recv()
        one, two = msg[b, c].astype(F32), xr[b].astype(F32)

        def aux_of(m):
            return m[:, latent : latent + 1], m[:, latent + 1 : latent + 2] + m[:, latent + 2 : latent + 3]

        (top1, sum1), (top2, sum2) = aux_of(one), aux_of(two)
        top = jnp.maximum(top1, top2)
        f1, f2 = jnp.exp2((top1 - top) * RATE), jnp.exp2((top2 - top) * RATE)
        inv = 1.0 / (f1 * sum1 + f2 * sum2)
        att = (f1 * inv) * one[:, 0:latent] + (f2 * inv) * two[:, 0:latent]
        att = att.reshape(n_exp, per_dev, latent)
        if not last:
            atf[...] = att
        else:
            ats[pair] = jnp.concatenate([atf[...], att], axis=1).astype(BF16)
            ar[e, pair] = ats[pair, e]
            each(1, n_exp, lambda d: att_copy(pair, d).start())

    def row_step(b):
        attend(b)

        @pl.when(b < rows - 2)
        def _():
            cache_copy(b + 2).start()

        @pl.when(b == 1)
        def _():
            merge(0, 0, False)
            for w in weight_copies[0:3]:
                w.start()

        @pl.when(b == 2)
        def _():
            merge(1, 0, True)
            for w in weight_copies[3:5]:
                w.start()

        @pl.when(b == 3)
        def _():
            merge(2, 1, False)
            weight_copies[5].start()

    each(0, rows, row_step)
    merge(3, 1, True)

    weight_copies[0].wait()
    for pair in range(2):
        each(1, n_exp, lambda d: att_copy(pair, d, True).wait_recv())
    n_rows = n_exp * rows
    x = ar[...].reshape(n_rows * per_dev, latent)
    for h in range(per_dev):
        v = mm(x, wv[h])
        v = jnp.where((iota(v.shape, 0) & (per_dev - 1)) == h, v, 0.0)
        v = jnp.sum(v.reshape(n_rows, per_dev, v.shape[1]), axis=1)
        vals[:, h * v.shape[1] : (h + 1) * v.shape[1]] = v.astype(BF16)

    def term_copy(k):
        return remote(osend.at[k], orecv.at[k], o_ss.at[k], o_rs.at[k], ctx=1 - c)

    weight_copies[1].wait()
    for k in range(4):
        osend[k] = mm(vals[...], wo[0, :, k * part : (k + 1) * part]).astype(BF16)
        term_copy(k).start()
    weight_copies[2].wait()
    for k in range(4):
        oown[k] = mm(vals[...], wo[1, :, k * part : (k + 1) * part])
    for k in range(4):
        term_copy(k).wait_recv()
        packed[k * n_rows : (k + 1) * n_rows, :] = (oown[k] + orecv[k].astype(F32)).astype(BF16)
    shape = (4 * n_rows, 4 * n_rows)
    i, j = iota(shape, 0), iota(shape, 1)
    spread = onehot(j == (((i & 15) >> 2) * n_rows + (i >> 4) * 4 + (i & 3)))
    rsend[...] = mm(spread, packed[...]).astype(BF16).reshape(n_exp, 16, part)
    rrecv[e] = rsend[e]

    def red_copy(d, back=False):
        to = lax.rem(e + d, n_exp)
        return remote(
            rsend.at[to], rrecv.at[to if back else e], r_ss.at[to], r_rs.at[to if back else e], exp=to
        )

    each(1, n_exp, lambda d: red_copy(d).start())
    wide = stream[...].astype(F32)
    base = jnp.concatenate([wide[:, k * part : (k + 1) * part] for k in range(4)], axis=0)
    each(1, n_exp, lambda d: red_copy(d, True).wait_recv())
    hidden = (base + jnp.sum(rrecv[...].astype(F32), axis=0)).astype(BF16)
    blocks[g] = hidden

    def pass_on(number, sem, row=None, exp=None):
        return remote(blocks.at[number], blocks.at[number], g_ss.at[sem], g_rs.at[number], row=row, exp=exp)

    def arrive(number):
        remote(blocks.at[number], blocks.at[number], g_ss.at[15], g_rs.at[number], row=1 - r).wait_recv()

    nz = n_exp // 2
    e_y = z * 2 + (1 - y)

    def own_z(d):
        pass_on(g, d - 1, exp=lax.rem(z + d, nz) * 2 + y).start()

    pass_on(g, 3, exp=e_y).start()
    each(1, nz, own_z)
    pass_on(g, 4, row=1 - r).start()

    def relay_z(d):
        number = r * n_exp + lax.rem(z + d, nz) * 2 + y
        arrive(number)
        pass_on(number, 4 + d, exp=e_y).start()
        pass_on(number, 7 + d, row=1 - r).start()

    each(1, nz, relay_z)

    def relay_y(d):
        number = r * n_exp + lax.rem(z + d, nz) * 2 + (1 - y)
        arrive(number)
        pass_on(number, 11 + d, row=1 - r).start()

    each(0, nz, relay_y)
    hw = hidden.astype(F32)
    for k in range(4):
        hid4[:, k * part : (k + 1) * part] = hw[4 * k : 4 * k + 4]
    each(1, devs, lambda d: tile_copy(d, True).wait_recv())
    slots_n = 2 * devs
    used = jnp.sum(trecv[...].reshape(devs // 4, 4, 8, 128), axis=1).reshape(slots_n, 128)
    used = jnp.concatenate([used, used], axis=1)
    line, col = iota(used.shape, 0), iota(used.shape, 1)
    used = (used > 0.0) & ((col >> 4) == (line >> 1))
    each(0, n_exp, lambda j: arrive((1 - r) * n_exp + j))

    sumsq = jnp.zeros((slots_n, 1), F32)
    flat = blocks[...].reshape(devs * 16, part)
    for k in range(4):
        xk = mm(onehot(used & (((col & 15) >> 2) == k)), flat)
        sumsq += jnp.sum(xk * xk, axis=1, keepdims=True)
        cut = slice(k * part, (k + 1) * part)
        xsel[:, cut] = (xk * gain[:, cut]).astype(BF16)
    sqsend[...] = jnp.broadcast_to(sumsq, sqsend.shape)
    sq = remote(sqsend, sqrecv, u_ss.at[2], u_rs.at[2], ctx=1 - c)
    sq.start()
    weight_copies[3].wait()
    weight_copies[4].wait()
    ffe = wg.shape[1]
    hf = ffe // 2

    def gu_copy(f):
        return remote(gusend.at[f], gurecv.at[f], u_ss.at[f], u_rs.at[f], ctx=1 - c)

    own = []
    for f in range(2):
        cut = slice(f * hf, (f + 1) * hf)
        gate, up = mm(xsel[...], wg[:, cut]), mm(xsel[...], wu[:, cut])
        own.append((gate, up))
        gusend[f, 0:slots_n] = gate.astype(BF16)
        gusend[f, slots_n : 2 * slots_n] = up.astype(BF16)
        gu_copy(f).start()
    sq.wait_recv()
    inverse = lax.rsqrt((sumsq + sqrecv[:, 0:1]) / D + epsilon)
    active = []
    for f in range(2):
        gu_copy(f).wait_recv()
        gate = inverse * (own[f][0] + gurecv[f, 0:slots_n].astype(F32))
        up = inverse * (own[f][1] + gurecv[f, slots_n : 2 * slots_n].astype(F32))
        active.append((gate / (1.0 + jnp.exp(-gate)) * up).astype(BF16))
    active = jnp.concatenate(active, axis=1)
    weight_copies[5].wait()
    for k in range(7):
        made[k * slots_n : (k + 1) * slots_n, :] = mm(active, wd[:, k * 512 : (k + 1) * 512]).astype(BF16)
    shape = (devs * 16, 7 * slots_n)
    i, j = iota(shape, 0), iota(shape, 1)
    spread = onehot(j == (((i & 15) >> 1) * slots_n + (i >> 4) * 2 + (i & 1)))
    psend[...] = mm(spread, made[...]).astype(BF16).reshape(devs, 16, 512)
    precv[g] = psend[g]

    def back_copy(d, back=False):
        to = lax.rem(g + d, devs)
        return remote(
            psend.at[to], precv.at[to if back else g], p_ss.at[to], p_rs.at[to if back else g],
            row=to // n_exp, exp=lax.rem(to, n_exp),
        )

    each(1, devs, lambda d: back_copy(d).start())

    each(1, devs, lambda d: tile_copy(d).wait_send())
    each(0, rows, lambda b: swap(b).wait_send())
    for pair in range(2):
        each(1, n_exp, lambda d: att_copy(pair, d).wait_send())
    for k in range(4):
        term_copy(k).wait_send()
    each(1, n_exp, lambda d: red_copy(d).wait_send())
    each(0, 15, lambda i: pass_on(g, i, row=1 - r).wait_send())
    sq.wait_send()
    for f in range(2):
        gu_copy(f).wait_send()

    each(1, devs, lambda d: back_copy(d, True).wait_recv())
    mix = mm(combine[...], precv[...].reshape(devs * 16, 512))
    mix = mix[0:32] + mix[32:64]
    for k in range(7):
        cut = slice(k * 512, (k + 1) * 512)
        out[:, cut] = (hid4[:, cut] + mix[4 * k : 4 * k + 4]).astype(BF16)
    each(1, devs, lambda d: back_copy(d).wait_send())


def fused(
    queries, latent_cache, lengths, w_value, w_out, stream, norm_gain, expert_ids, gate_weights,
    w_gate, w_up, w_down,
):
    rows, heads, qk = queries.shape
    block = latent_cache.shape[1]
    per_dev, latent, v_head = w_value.shape
    width = stream.shape[1]
    n_exp = lax.axis_size("exp")
    devs = n_exp * lax.axis_size("row")
    depth, ffe = w_out.shape[0], w_gate.shape[2]
    part, n_rows, slots_n = width // 4, n_exp * rows, 2 * devs
    vmem, smem, anyw = (pl.BlockSpec(memory_space=s) for s in (pltpu.VMEM, pltpu.SMEM, pl.ANY))
    dma = pltpu.SemaphoreType.DMA
    scratch = [
        pltpu.VMEM((2, block, qk), BF16),
        pltpu.VMEM(w_value.shape, BF16),
        pltpu.VMEM((2, depth, width), BF16),
        pltpu.VMEM((width, ffe), BF16),
        pltpu.VMEM((width, ffe), BF16),
        pltpu.VMEM((ffe, width), BF16),
        pltpu.VMEM((heads, block), F32),
        pltpu.VMEM((rows, 2, heads // 2, latent + 128), BF16),
        pltpu.VMEM((rows, heads // 2, latent + 128), BF16),
        pltpu.VMEM((n_exp, per_dev, latent), F32),
        pltpu.VMEM((2, n_exp, 16, latent), BF16),
        pltpu.VMEM((n_exp, 2, 16, latent), BF16),
        pltpu.VMEM((n_rows, depth), BF16),
        pltpu.VMEM((4, n_rows, part), BF16),
        pltpu.VMEM((4, n_rows, part), F32),
        pltpu.VMEM((4, n_rows, part), BF16),
        pltpu.VMEM((4 * n_rows, part), BF16),
        pltpu.VMEM((n_exp, 16, part), BF16),
        pltpu.VMEM((n_exp, 16, part), BF16),
        pltpu.VMEM((rows, width), F32),
        pltpu.VMEM((devs, 16, part), BF16),
        pltpu.VMEM((devs, 8, 128), F32),
        pltpu.VMEM((devs, 8, 128), F32),
        pltpu.VMEM((slots_n, width), BF16),
        pltpu.VMEM((2, 2 * slots_n, ffe // 2), BF16),
        pltpu.VMEM((2, 2 * slots_n, ffe // 2), BF16),
        pltpu.VMEM((slots_n, 128), F32),
        pltpu.VMEM((slots_n, 128), F32),
        pltpu.VMEM((7 * slots_n, 512), BF16),
        pltpu.VMEM((devs, 16, 512), BF16),
        pltpu.VMEM((devs, 16, 512), BF16),
        pltpu.VMEM((64, devs * 16), BF16),
    ] + [
        dma(s)
        for s in (
            (2,), (6,), (rows,), (rows,), (2, n_exp), (2, n_exp), (4,), (4,), (n_exp,), (n_exp,),
            (16,), (devs,), (devs,), (devs,), (3,), (3,), (devs,), (devs,),
        )
    ]
    return pl.pallas_call(
        layer_kernel,
        out_shape=jax.ShapeDtypeStruct((rows, width), BF16),
        in_specs=[vmem, anyw, smem, anyw, anyw, vmem, vmem, smem, smem, anyw, anyw, anyw],
        out_specs=vmem,
        scratch_shapes=scratch,
        compiler_params=pltpu.CompilerParams(
            collective_id=0, has_side_effects=True, vmem_limit_bytes=60 * 1024 * 1024
        ),
    )(
        queries, latent_cache, lengths, w_value, w_out, stream, norm_gain[None, :], expert_ids,
        gate_weights, w_gate, w_up, w_down,
    )


def solution(mesh):
    placed = (
        P(("row", "exp"), None, None),
        P(("row", "exp"), "ctx", None),
        P(("row", "exp")),
        P(("ctx", "exp"), None, None),
        P(("ctx", "exp"), None),
        P(("row", "exp"), "ctx"),
        P("ctx"),
        P(("row", "exp"), None),
        P(("row", "exp"), None),
        P(("row", "exp"), "ctx", None),
        P(("row", "exp"), "ctx", None),
        P(("row", "exp"), None, "ctx"),
    )
    sizes = tuple(mesh.shape[axis] for axis in ("ctx", "row", "exp"))
    body = fused if sizes == (2, 2, 8) else on_device
    return jax.shard_map(
        body, mesh=mesh, in_specs=placed, out_specs=P(("row", "exp"), "ctx"), check_vma=False
    )
```

```python
import math

import jax
import jax.numpy as jnp
from jax import lax
from jax.experimental import pallas as pl
from jax.experimental.pallas import tpu as pltpu
from jax.sharding import PartitionSpec as P

D = 7168
QK_HEAD = 192


epsilon = 1e-06


def merge_blocks(outputs, maxima, totals):
    top_value = jnp.max(maxima, axis=0)
    factor = jnp.exp(maxima - top_value[None])
    numer = jnp.sum(factor[..., None] * outputs, axis=0)
    denom = jnp.sum(factor * totals, axis=0)
    return (numer / denom[..., None]).astype(jnp.bfloat16)


def on_device(
    queries,
    latent_cache,
    lengths,
    w_value,
    w_out,
    stream,
    norm_gain,
    expert_ids,
    gate_weights,
    w_gate,
    w_up,
    w_down,
):
    n_ctx = lax.axis_size("ctx")
    n_row = lax.axis_size("row")
    n_exp = lax.axis_size("exp")
    groups = queries.shape[0]
    block = latent_cache.shape[1]
    per_dev = w_value.shape[0]
    latent = w_value.shape[1]
    scores = jnp.einsum(
        "bhw,btw->bht", queries, latent_cache, preferred_element_type=jnp.float32
    ) * QK_HEAD ** (-0.5)
    position = lax.axis_index("ctx") * block + jnp.arange(block, dtype=jnp.int32)
    live = (position[None, :] < lengths[:, None])[:, None, :]
    block_max = jnp.max(jnp.where(live, scores, -jnp.inf), axis=2)
    shift_by = jnp.where(jnp.isfinite(block_max), block_max, 0.0)
    weights = jnp.where(live, jnp.exp(scores - shift_by[..., None]), 0.0)
    totals = jnp.sum(weights, axis=2)
    latent_out = jnp.einsum(
        "bht,btl->bhl",
        weights.astype(jnp.bfloat16),
        latent_cache[:, :, :latent],
        preferred_element_type=jnp.float32,
    )
    outputs, maxima, sums = (
        lax.all_to_all(
            latent_out.reshape(1, groups, n_ctx * n_exp, per_dev, latent),
            ("ctx", "exp"),
            split_axis=2,
            concat_axis=0,
            tiled=True,
        ),
        lax.all_to_all(
            block_max.reshape(1, groups, n_ctx * n_exp, per_dev),
            ("ctx", "exp"),
            split_axis=2,
            concat_axis=0,
            tiled=True,
        ),
        lax.all_to_all(
            totals.reshape(1, groups, n_ctx * n_exp, per_dev),
            ("ctx", "exp"),
            split_axis=2,
            concat_axis=0,
            tiled=True,
        ),
    )
    gathered_rows = n_exp * groups
    attended = merge_blocks(
        outputs.reshape(n_ctx, gathered_rows, per_dev, latent),
        maxima.reshape(n_ctx, gathered_rows, per_dev),
        sums.reshape(n_ctx, gathered_rows, per_dev),
    )
    values = jnp.einsum("nhl,hlv->nhv", attended, w_value, preferred_element_type=jnp.float32)
    values = values.astype(jnp.bfloat16).reshape(gathered_rows, -1)
    split_out = w_out.reshape(w_out.shape[0], n_ctx, -1)
    term_rows = jnp.einsum(
        "nk,kcd->cnd", values, split_out, preferred_element_type=jnp.float32
    ).reshape(n_ctx * gathered_rows, -1)
    attn_out = lax.psum_scatter(term_rows, ("ctx", "exp"), scatter_dimension=0, tiled=True)
    hidden = lax.optimization_barrier((stream.astype(jnp.float32) + attn_out).astype(jnp.bfloat16))
    experts = n_row * n_exp
    picks = expert_ids.shape[1]
    capacity = max(2, (groups * picks + experts - 1) // experts)
    expert_range = jnp.arange(experts, dtype=jnp.int32)
    onehot = expert_ids[:, :, None] == expert_range[None, None, :]
    named = jnp.sum(onehot.astype(jnp.int32), axis=1)
    slot_of = jnp.cumsum(named, axis=0) - named
    slot_match = slot_of[:, :, None] == jnp.arange(capacity, dtype=jnp.int32)[None, None, :]
    placed = (named[:, :, None] == 1) & slot_match
    outgoing = jnp.einsum(
        "bxs,bd->xsd", placed.astype(jnp.bfloat16), hidden, preferred_element_type=jnp.float32
    ).astype(jnp.bfloat16)
    width_dev = outgoing.shape[2]
    arrived = lax.all_to_all(outgoing, ("row", "exp"), split_axis=0, concat_axis=0, tiled=True)
    arrived = arrived.reshape(experts * capacity, width_dev)
    arrived_wide = arrived.astype(jnp.float32)
    sumsq = jnp.sum(arrived_wide * arrived_wide, axis=1)
    scaled = (arrived_wide * norm_gain[None, :]).astype(jnp.bfloat16)
    gate_part = jnp.dot(scaled, w_gate[0], preferred_element_type=jnp.float32)
    up_part = jnp.dot(scaled, w_up[0], preferred_element_type=jnp.float32)
    gate_part, up_part, sumsq = lax.psum((gate_part, up_part, sumsq), "ctx")
    inverse = lax.rsqrt(sumsq / D + epsilon)[:, None]
    active = (jax.nn.silu(inverse * gate_part) * (inverse * up_part)).astype(jnp.bfloat16)
    produced = jnp.dot(active, w_down[0], preferred_element_type=jnp.float32).astype(jnp.bfloat16)
    returned = lax.all_to_all(
        produced.reshape(experts, capacity, width_dev),
        ("row", "exp"),
        split_axis=0,
        concat_axis=0,
        tiled=True,
    )
    weighted = jnp.sum(gate_weights[:, :, None] * onehot.astype(jnp.float32), axis=1)
    combine = weighted[:, :, None] * slot_match.astype(jnp.float32)
    mixture = jnp.einsum(
        "bxs,xsd->bd", combine, returned.astype(jnp.float32), precision=lax.Precision.HIGHEST
    )
    return (hidden.astype(jnp.float32) + mixture).astype(jnp.bfloat16)


F32 = jnp.float32
BF16 = jnp.bfloat16
MESH = pl.DeviceIdType.MESH
DEAD = -1e30
FLOOR = -1e29
RATE = QK_HEAD ** (-0.5) * math.log2(math.e)


def iota(shape, dim):
    return lax.broadcasted_iota(jnp.int32, shape, dim)


def mm(a, b):
    return jnp.dot(a, b, preferred_element_type=F32)


def onehot(cond):
    return jnp.where(cond, 1.0, 0.0).astype(BF16)


def routing(expert, ids, gates, rows, picks):
    weights, slots = [], []
    before = jnp.zeros(expert.shape, jnp.int32)
    for b in range(rows):
        weight = jnp.zeros(expert.shape, F32)
        for k in range(picks):
            weight = jnp.where(expert == ids[b, k], gates[b, k], weight)
        weights.append(weight)
        slots.append(before)
        before = before + jnp.where(weight > 0.0, 1, 0)
    return weights, slots


def layer_kernel(
    queries, cache_hbm, lengths, wv_hbm, wo_hbm, stream, gain, ids, gates, wg_hbm, wu_hbm, wd_hbm,
    out,
    cache, wv, wo, wg, wu, wd,
    scores, msg, xr, ats, ar, vals, osend0, oown0, orecv0, rsend0, rrecv0, osend1, oown1, orecv1, rsend1, rrecv1, hid4, blocks,
    tsend, trecv, xsel, gusend, gurecv, sqsend, sqrecv, made, psend, precv, combine,
    cache_sem, w_sem, x_ss, x_rs, a_ss, a_rs, o_ss, o_rs, r_ss, r_rs, g_ss, g_rs, t_ss, t_rs,
    u_ss, u_rs, p_ss, p_rs,
):
    rows, _, heads = queries.shape
    block = cache_hbm.shape[2]
    latent = wv_hbm.shape[1]
    n_exp = lax.axis_size("exp")
    devs = lax.axis_size("row") * n_exp
    picks = ids.shape[1]
    per_dev = wv_hbm.shape[0]
    width = stream.shape[1]
    part, w0 = width // 4, 512
    w1 = part - w0
    c, r, e = lax.axis_index("ctx"), lax.axis_index("row"), lax.axis_index("exp")
    g = r * n_exp + e
    z, y = e // 2, lax.rem(e, 2)
    half_heads = heads // 2

    def remote(src, dst, ss, rs, ctx=None, row=None, exp=None):
        where = {
            "ctx": c if ctx is None else ctx,
            "row": r if row is None else row,
            "exp": e if exp is None else exp,
        }
        return pltpu.make_async_remote_copy(
            src_ref=src, dst_ref=dst, send_sem=ss, recv_sem=rs, device_id=where, device_id_type=MESH
        )

    def each(low, high, body):
        def step(i, carry):
            body(i)
            return carry

        lax.fori_loop(low, high, step, 0)

    def cache_copy(b):
        slot = lax.rem(b, 2)
        return pltpu.make_async_copy(cache_hbm.at[b], cache.at[slot], cache_sem.at[slot])

    def half_of(i):
        side = (1 - c) if i == 0 else c
        return wo_hbm.at[:, pl.ds(pl.multiple_of(side * width, 128), width)]

    weight_copies = [
        pltpu.make_async_copy(wv_hbm, wv, w_sem.at[0]),
        pltpu.make_async_copy(half_of(0), wo.at[0], w_sem.at[1]),
        pltpu.make_async_copy(half_of(1), wo.at[1], w_sem.at[2]),
        pltpu.make_async_copy(wg_hbm.at[0], wg, w_sem.at[3]),
        pltpu.make_async_copy(wu_hbm.at[0], wu, w_sem.at[4]),
        pltpu.make_async_copy(wd_hbm.at[0], wd, w_sem.at[5]),
    ]

    cache_copy(0).start()
    cache_copy(1).start()

    barrier = pltpu.get_barrier_semaphore()
    pl.semaphore_signal(
        barrier, inc=1, device_id={"ctx": 1 - c, "row": r, "exp": e}, device_id_type=MESH
    )

    def greet(d):
        to = lax.rem(g + d, devs)
        pl.semaphore_signal(
            barrier, inc=1, device_id={"ctx": c, "row": to // n_exp, "exp": lax.rem(to, n_exp)},
            device_id_type=MESH,
        )

    each(1, devs, greet)

    pl.semaphore_wait(barrier, devs)

    def tile_copy(d, back=False):
        to = lax.rem(g + d, devs)
        return remote(
            tsend.at[to], trecv.at[to if back else g], t_ss.at[to], t_rs.at[to if back else g],
            row=to // n_exp, exp=lax.rem(to, n_exp),
        )

    def swap(b):
        return remote(msg.at[b, 1 - c], xr.at[b], x_ss.at[b], x_rs.at[b], ctx=1 - c)

    def att_copy(b, d, back=False):
        to = lax.rem(e + d, n_exp)
        return remote(
            ats.at[b, to], ar.at[to if back else e, b],
            a_ss.at[b, to], a_rs.at[b, to if back else e], exp=to,
        )

    def attend(b):
        slot = lax.rem(b, 2)
        cache_copy(b).wait()
        query = queries[b].T
        live = lengths[b] - c * block
        step = 1024
        tops = []
        for t in range(block // step):
            span = slice(t * step, (t + 1) * step)
            s = mm(query, cache[slot, :, span])
            s = jnp.where(iota(s.shape, 1) + t * step < live, s, DEAD)
            scores[:, span] = s
            tops.append(jnp.max(s, axis=1, keepdims=True))
        top = tops[0]
        for other in tops[1:]:
            top = jnp.maximum(top, other)
        top = jnp.maximum(top, FLOOR).astype(BF16).astype(F32)
        total = jnp.zeros_like(top)
        acc = jnp.zeros((heads, latent), F32)
        for t in range(block // step):
            span = slice(t * step, (t + 1) * step)
            p = jnp.exp2((scores[:, span] - top) * RATE)
            total += jnp.sum(p, axis=1, keepdims=True)
            acc += lax.dot_general(
                p.astype(BF16), cache[slot, 0:latent, span], (((1,), (1,)), ((), ())),
                preferred_element_type=F32,
            )
        lane = iota((heads, 128), 1)
        rest = total - total.astype(BF16).astype(F32)
        aux = jnp.where(lane == 0, top, jnp.where(lane == 1, total, jnp.where(lane == 2, rest, 0.0)))
        acc, aux = acc.astype(BF16), aux.astype(BF16)
        for side in range(2):
            mine = slice(side * half_heads, (side + 1) * half_heads)
            msg[b, side, :, 0:latent] = acc[mine]
            msg[b, side, :, latent : latent + 128] = aux[mine]
        swap(b).start()

    def merge(b):
        swap(b).wait_recv()
        one, two = msg[b, c].astype(F32), xr[b].astype(F32)

        def aux_of(m):
            return m[:, latent : latent + 1], m[:, latent + 1 : latent + 2] + m[:, latent + 2 : latent + 3]

        (top1, sum1), (top2, sum2) = aux_of(one), aux_of(two)
        top = jnp.maximum(top1, top2)
        f1, f2 = jnp.exp2((top1 - top) * RATE), jnp.exp2((top2 - top) * RATE)
        inv = 1.0 / (f1 * sum1 + f2 * sum2)
        att = (f1 * inv) * one[:, 0:latent] + (f2 * inv) * two[:, 0:latent]
        att = att.reshape(n_exp, per_dev, latent)
        half = latent // 2
        ats[b] = jnp.concatenate([att[:, :, 0:half], att[:, :, half:]], axis=1).astype(BF16)
        ar[e, b] = ats[b, e]
        each(1, n_exp, lambda d: att_copy(b, d).start())

    def row_step(b):
        attend(b)

        @pl.when(b < rows - 2)
        def _():
            cache_copy(b + 2).start()

        @pl.when(b == 1)
        def _():
            merge(0)
            for w in weight_copies[0:3]:
                w.start()

        @pl.when(b == 2)
        def _():
            merge(1)
            for w in weight_copies[3:5]:
                w.start()

        @pl.when(b == 3)
        def _():
            merge(2)
            weight_copies[5].start()

    each(0, rows, row_step)
    merge(3)

    shape = (devs, 8, 128)
    expert, sub, lane = iota(shape, 0), iota(shape, 1), iota(shape, 2)
    weights, slots = routing(expert, ids, gates, rows, picks)
    tile = jnp.zeros(shape, F32)
    for b in range(rows):
        here = ((lane & 3) == b) & (sub == 2 * lax.rem(g, 4) + slots[b])
        tile = jnp.where(here, weights[b], tile)
    tsend[...] = tile
    trecv[g] = tsend[g]
    each(1, devs, lambda d: tile_copy(d).start())

    weight_copies[0].wait()
    for b in range(rows):
        each(1, n_exp, lambda d: att_copy(b, d, True).wait_recv())
    n_rows = n_exp * rows
    x = ar[...].astype(F32).reshape(n_rows, 2, per_dev, latent // 2)
    x = jnp.concatenate([x[:, 0], x[:, 1]], axis=2).reshape(n_rows * per_dev, latent).astype(BF16)
    for h in range(per_dev):
        v = mm(x, wv[h])
        v = jnp.where((iota(v.shape, 0) & (per_dev - 1)) == h, v, 0.0)
        v = jnp.sum(v.reshape(n_rows, per_dev, v.shape[1]), axis=1)
        vals[:, h * v.shape[1] : (h + 1) * v.shape[1]] = v.astype(BF16)

    def cuts(k):
        return slice(k * w0, (k + 1) * w0), slice(4 * w0 + k * w1, 4 * w0 + (k + 1) * w1)

    osend, oown, orecv, rsend, rrecv = (osend0, osend1), (oown0, oown1), (orecv0, orecv1), (rsend0, rsend1), (rrecv0, rrecv1)

    def term_copy(q):
        return remote(osend[q], orecv[q], o_ss.at[q], o_rs.at[q], ctx=1 - c)

    def red_copy(q, d, back=False):
        to = lax.rem(e + d, n_exp)
        return remote(
            rsend[q].at[to], rrecv[q].at[to if back else e],
            r_ss.at[q, to], r_rs.at[q, to if back else e], exp=to,
        )

    weight_copies[1].wait()
    for q in range(2):
        for k in range(4):
            osend[q][k] = mm(vals[...], wo[0, :, cuts(k)[q]]).astype(BF16)
        term_copy(q).start()
    weight_copies[2].wait()
    shape = (4 * n_rows, 4 * n_rows)
    i, j = iota(shape, 0), iota(shape, 1)
    spread = onehot(j == (((i & 15) >> 2) * n_rows + (i >> 4) * 4 + (i & 3)))
    for q in range(2):
        for k in range(4):
            oown[q][k] = mm(vals[...], wo[1, :, cuts(k)[q]])
    for q in range(2):
        term_copy(q).wait_recv()
        both = oown[q][...] + orecv[q][...].astype(F32)
        both = both.reshape(4 * n_rows, both.shape[2]).astype(BF16)
        rsend[q][...] = mm(spread, both).astype(BF16).reshape(rsend[q].shape)
        rrecv[q][e] = rsend[q][e]
        each(1, n_exp, lambda d: red_copy(q, d).start())
    wide = stream[...].astype(F32)
    base = jnp.concatenate(
        [jnp.concatenate([wide[:, cut] for cut in cuts(k)], axis=1) for k in range(4)], axis=0
    )
    for q in range(2):
        each(1, n_exp, lambda d: red_copy(q, d, True).wait_recv())
    attn = jnp.concatenate([jnp.sum(rrecv[q][...].astype(F32), axis=0) for q in range(2)], axis=1)
    hidden = (base + attn).astype(BF16)
    blocks[g] = hidden

    def pass_on(number, sem, row=None, exp=None):
        return remote(blocks.at[number], blocks.at[number], g_ss.at[sem], g_rs.at[number], row=row, exp=exp)

    def arrive(number):
        remote(blocks.at[number], blocks.at[number], g_ss.at[15], g_rs.at[number], row=1 - r).wait_recv()

    nz = n_exp // 2
    e_y = z * 2 + (1 - y)

    def own_z(d):
        pass_on(g, d - 1, exp=lax.rem(z + d, nz) * 2 + y).start()

    pass_on(g, 3, exp=e_y).start()
    each(1, nz, own_z)
    pass_on(g, 4, row=1 - r).start()

    def relay_z(d):
        number = r * n_exp + lax.rem(z + d, nz) * 2 + y
        arrive(number)
        pass_on(number, 4 + d, exp=e_y).start()
        pass_on(number, 7 + d, row=1 - r).start()

    each(1, nz, relay_z)

    def relay_y(d):
        number = r * n_exp + lax.rem(z + d, nz) * 2 + (1 - y)
        arrive(number)
        pass_on(number, 11 + d, row=1 - r).start()

    each(0, nz, relay_y)
    hw = hidden.astype(F32)
    for k in range(4):
        for cut, lanes in zip(cuts(k), (slice(0, w0), slice(w0, part))):
            hid4[:, cut] = hw[4 * k : 4 * k + 4, lanes]
    each(1, devs, lambda d: tile_copy(d, True).wait_recv())
    slots_n = 2 * devs
    used = jnp.sum(trecv[...].reshape(devs // 4, 4, 8, 128), axis=1).reshape(slots_n, 128)
    used = jnp.concatenate([used, used], axis=1)
    line, col = iota(used.shape, 0), iota(used.shape, 1)
    used = (used > 0.0) & ((col >> 4) == (line >> 1))
    each(0, n_exp, lambda j: arrive((1 - r) * n_exp + j))

    sumsq = jnp.zeros((slots_n, 1), F32)
    scale = gain[...].reshape(1, width)
    flat = blocks[...].reshape(devs * 16, part)
    for k in range(4):
        xk = mm(onehot(used & (((col & 15) >> 2) == k)), flat)
        sumsq += jnp.sum(xk * xk, axis=1, keepdims=True)
        for cut, lanes in zip(cuts(k), (slice(0, w0), slice(w0, part))):
            xsel[:, cut] = (xk[:, lanes] * scale[:, cut]).astype(BF16)
    sqsend[...] = jnp.broadcast_to(sumsq, sqsend.shape)
    sq = remote(sqsend, sqrecv, u_ss.at[2], u_rs.at[2], ctx=1 - c)
    sq.start()
    weight_copies[3].wait()
    weight_copies[4].wait()
    ffe = wg.shape[1]
    hf = ffe // 2

    def gu_copy(f):
        return remote(gusend.at[f], gurecv.at[f], u_ss.at[f], u_rs.at[f], ctx=1 - c)

    own = []
    for f in range(2):
        cut = slice(f * hf, (f + 1) * hf)
        gate, up = mm(xsel[...], wg[:, cut]), mm(xsel[...], wu[:, cut])
        own.append((gate, up))
        gusend[f, 0:slots_n] = gate.astype(BF16)
        gusend[f, slots_n : 2 * slots_n] = up.astype(BF16)
        gu_copy(f).start()
    sq.wait_recv()
    inverse = lax.rsqrt((sumsq + sqrecv[:, 0:1]) / D + epsilon)
    active = []
    for f in range(2):
        gu_copy(f).wait_recv()
        gate = inverse * (own[f][0] + gurecv[f, 0:slots_n].astype(F32))
        up = inverse * (own[f][1] + gurecv[f, slots_n : 2 * slots_n].astype(F32))
        active.append((gate / (1.0 + jnp.exp(-gate)) * up).astype(BF16))
    active = jnp.concatenate(active, axis=1)
    weight_copies[5].wait()
    for k in range(7):
        made[k * slots_n : (k + 1) * slots_n, :] = mm(active, wd[:, k * 512 : (k + 1) * 512]).astype(BF16)
    shape = (devs * 16, 7 * slots_n)
    i, j = iota(shape, 0), iota(shape, 1)
    spread = onehot(j == (((i & 15) >> 1) * slots_n + (i >> 4) * 2 + (i & 1)))
    psend[...] = mm(spread, made[...]).astype(BF16).reshape(devs, 16, 512)
    precv[g] = psend[g]

    def back_copy(d, back=False):
        to = lax.rem(g + d, devs)
        return remote(
            psend.at[to], precv.at[to if back else g], p_ss.at[to], p_rs.at[to if back else g],
            row=to // n_exp, exp=lax.rem(to, n_exp),
        )

    each(1, devs, lambda d: back_copy(d).start())

    shape = (32, devs * 16)
    line, col = iota(shape, 0), iota(shape, 1)
    weights, slots = routing(col >> 4, ids, gates, rows, picks)
    comb = jnp.zeros(shape, F32)
    for b in range(rows):
        here = ((line & 3) == b) & ((line >> 2) == ((col & 15) >> 1)) & ((col & 1) == slots[b])
        comb = jnp.where(here, weights[b], comb)
    high = comb.astype(BF16)
    combine[0:32, :] = high
    combine[32:64, :] = (comb - high.astype(F32)).astype(BF16)

    each(1, devs, lambda d: tile_copy(d).wait_send())
    each(0, rows, lambda b: swap(b).wait_send())
    for b in range(rows):
        each(1, n_exp, lambda d: att_copy(b, d).wait_send())
    for q in range(2):
        term_copy(q).wait_send()
        each(1, n_exp, lambda d: red_copy(q, d).wait_send())
    each(0, 15, lambda i: pass_on(g, i, row=1 - r).wait_send())
    sq.wait_send()
    for f in range(2):
        gu_copy(f).wait_send()

    each(1, devs, lambda d: back_copy(d, True).wait_recv())
    mix = mm(combine[...], precv[...].reshape(devs * 16, 512))
    mix = mix[0:32] + mix[32:64]
    for k in range(7):
        cut = slice(k * 512, (k + 1) * 512)
        out[:, cut] = (hid4[:, cut] + mix[4 * k : 4 * k + 4]).astype(BF16)
    each(1, devs, lambda d: back_copy(d).wait_send())


def fused(
    queries, latent_cache, lengths, w_value, w_out, stream, norm_gain, expert_ids, gate_weights,
    w_gate, w_up, w_down,
):
    rows, heads, qk = queries.shape
    block = latent_cache.shape[1]
    per_dev, latent, v_head = w_value.shape
    width = stream.shape[1]
    n_exp = lax.axis_size("exp")
    devs = n_exp * lax.axis_size("row")
    depth, ffe = w_out.shape[0], w_gate.shape[2]
    part, n_rows, slots_n = width // 4, n_exp * rows, 2 * devs
    vmem, smem, anyw = (pl.BlockSpec(memory_space=s) for s in (pltpu.VMEM, pltpu.SMEM, pl.ANY))
    dma = pltpu.SemaphoreType.DMA
    scratch = [
        pltpu.VMEM((2, qk, block), BF16),
        pltpu.VMEM(w_value.shape, BF16),
        pltpu.VMEM((2, depth, width), BF16),
        pltpu.VMEM((width, ffe), BF16),
        pltpu.VMEM((width, ffe), BF16),
        pltpu.VMEM((ffe, width), BF16),
        pltpu.VMEM((heads, block), F32),
        pltpu.VMEM((rows, 2, heads // 2, latent + 128), BF16),
        pltpu.VMEM((rows, heads // 2, latent + 128), BF16),
        pltpu.VMEM((rows, n_exp, 16, latent // 2), BF16),
        pltpu.VMEM((n_exp, rows, 16, latent // 2), BF16),
        pltpu.VMEM((n_rows, depth), BF16),
        *(
            buffer
            for piece in (512, part - 512)
            for buffer in (
                pltpu.VMEM((4, n_rows, piece), BF16),
                pltpu.VMEM((4, n_rows, piece), F32),
                pltpu.VMEM((4, n_rows, piece), BF16),
                pltpu.VMEM((n_exp, 16, piece), BF16),
                pltpu.VMEM((n_exp, 16, piece), BF16),
            )
        ),
        pltpu.VMEM((rows, width), F32),
        pltpu.VMEM((devs, 16, part), BF16),
        pltpu.VMEM((devs, 8, 128), F32),
        pltpu.VMEM((devs, 8, 128), F32),
        pltpu.VMEM((slots_n, width), BF16),
        pltpu.VMEM((2, 2 * slots_n, ffe // 2), BF16),
        pltpu.VMEM((2, 2 * slots_n, ffe // 2), BF16),
        pltpu.VMEM((slots_n, 128), F32),
        pltpu.VMEM((slots_n, 128), F32),
        pltpu.VMEM((7 * slots_n, 512), BF16),
        pltpu.VMEM((devs, 16, 512), BF16),
        pltpu.VMEM((devs, 16, 512), BF16),
        pltpu.VMEM((64, devs * 16), BF16),
    ] + [
        dma(s)
        for s in (
            (2,), (6,), (rows,), (rows,), (rows, n_exp), (rows, n_exp), (2,), (2,), (2, n_exp), (2, n_exp),
            (16,), (devs,), (devs,), (devs,), (3,), (3,), (devs,), (devs,),
        )
    ]
    return pl.pallas_call(
        layer_kernel,
        out_shape=jax.ShapeDtypeStruct((rows, width), BF16),
        in_specs=[vmem, anyw, smem, anyw, anyw, vmem, vmem, smem, smem, anyw, anyw, anyw],
        out_specs=vmem,
        scratch_shapes=scratch,
        compiler_params=pltpu.CompilerParams(
            collective_id=0, has_side_effects=True, vmem_limit_bytes=60 * 1024 * 1024
        ),
    )(
        jnp.swapaxes(queries, 1, 2), jnp.swapaxes(latent_cache, 1, 2), lengths, w_value, w_out, stream,
        norm_gain, expert_ids, gate_weights, w_gate, w_up, w_down,
    )


def solution(mesh):
    placed = (
        P(("row", "exp"), None, None),
        P(("row", "exp"), "ctx", None),
        P(("row", "exp")),
        P(("ctx", "exp"), None, None),
        P(("ctx", "exp"), None),
        P(("row", "exp"), "ctx"),
        P("ctx"),
        P(("row", "exp"), None),
        P(("row", "exp"), None),
        P(("row", "exp"), "ctx", None),
        P(("row", "exp"), "ctx", None),
        P(("row", "exp"), None, "ctx"),
    )
    sizes = tuple(mesh.shape[axis] for axis in ("ctx", "row", "exp"))
    body = fused if sizes == (2, 2, 8) else on_device
    return jax.shard_map(
        body, mesh=mesh, in_specs=placed, out_specs=P(("row", "exp"), "ctx"), check_vma=False
    )
```

```python
import math

import jax
import jax.numpy as jnp
from jax import lax
from jax.experimental import pallas as pl
from jax.experimental.pallas import tpu as pltpu
from jax.sharding import PartitionSpec as P

D = 7168
QK_HEAD = 192


epsilon = 1e-06


def merge_blocks(outputs, maxima, totals):
    top_value = jnp.max(maxima, axis=0)
    factor = jnp.exp(maxima - top_value[None])
    numer = jnp.sum(factor[..., None] * outputs, axis=0)
    denom = jnp.sum(factor * totals, axis=0)
    return (numer / denom[..., None]).astype(jnp.bfloat16)


def on_device(
    queries,
    latent_cache,
    lengths,
    w_value,
    w_out,
    stream,
    norm_gain,
    expert_ids,
    gate_weights,
    w_gate,
    w_up,
    w_down,
):
    n_ctx = lax.axis_size("ctx")
    n_row = lax.axis_size("row")
    n_exp = lax.axis_size("exp")
    groups = queries.shape[0]
    block = latent_cache.shape[1]
    per_dev = w_value.shape[0]
    latent = w_value.shape[1]
    scores = jnp.einsum(
        "bhw,btw->bht", queries, latent_cache, preferred_element_type=jnp.float32
    ) * QK_HEAD ** (-0.5)
    position = lax.axis_index("ctx") * block + jnp.arange(block, dtype=jnp.int32)
    live = (position[None, :] < lengths[:, None])[:, None, :]
    block_max = jnp.max(jnp.where(live, scores, -jnp.inf), axis=2)
    shift_by = jnp.where(jnp.isfinite(block_max), block_max, 0.0)
    weights = jnp.where(live, jnp.exp(scores - shift_by[..., None]), 0.0)
    totals = jnp.sum(weights, axis=2)
    latent_out = jnp.einsum(
        "bht,btl->bhl",
        weights.astype(jnp.bfloat16),
        latent_cache[:, :, :latent],
        preferred_element_type=jnp.float32,
    )
    outputs, maxima, sums = (
        lax.all_to_all(
            latent_out.reshape(1, groups, n_ctx * n_exp, per_dev, latent),
            ("ctx", "exp"),
            split_axis=2,
            concat_axis=0,
            tiled=True,
        ),
        lax.all_to_all(
            block_max.reshape(1, groups, n_ctx * n_exp, per_dev),
            ("ctx", "exp"),
            split_axis=2,
            concat_axis=0,
            tiled=True,
        ),
        lax.all_to_all(
            totals.reshape(1, groups, n_ctx * n_exp, per_dev),
            ("ctx", "exp"),
            split_axis=2,
            concat_axis=0,
            tiled=True,
        ),
    )
    gathered_rows = n_exp * groups
    attended = merge_blocks(
        outputs.reshape(n_ctx, gathered_rows, per_dev, latent),
        maxima.reshape(n_ctx, gathered_rows, per_dev),
        sums.reshape(n_ctx, gathered_rows, per_dev),
    )
    values = jnp.einsum("nhl,hlv->nhv", attended, w_value, preferred_element_type=jnp.float32)
    values = values.astype(jnp.bfloat16).reshape(gathered_rows, -1)
    split_out = w_out.reshape(w_out.shape[0], n_ctx, -1)
    term_rows = jnp.einsum(
        "nk,kcd->cnd", values, split_out, preferred_element_type=jnp.float32
    ).reshape(n_ctx * gathered_rows, -1)
    attn_out = lax.psum_scatter(term_rows, ("ctx", "exp"), scatter_dimension=0, tiled=True)
    hidden = lax.optimization_barrier((stream.astype(jnp.float32) + attn_out).astype(jnp.bfloat16))
    experts = n_row * n_exp
    picks = expert_ids.shape[1]
    capacity = max(2, (groups * picks + experts - 1) // experts)
    expert_range = jnp.arange(experts, dtype=jnp.int32)
    onehot = expert_ids[:, :, None] == expert_range[None, None, :]
    named = jnp.sum(onehot.astype(jnp.int32), axis=1)
    slot_of = jnp.cumsum(named, axis=0) - named
    slot_match = slot_of[:, :, None] == jnp.arange(capacity, dtype=jnp.int32)[None, None, :]
    placed = (named[:, :, None] == 1) & slot_match
    outgoing = jnp.einsum(
        "bxs,bd->xsd", placed.astype(jnp.bfloat16), hidden, preferred_element_type=jnp.float32
    ).astype(jnp.bfloat16)
    width_dev = outgoing.shape[2]
    arrived = lax.all_to_all(outgoing, ("row", "exp"), split_axis=0, concat_axis=0, tiled=True)
    arrived = arrived.reshape(experts * capacity, width_dev)
    arrived_wide = arrived.astype(jnp.float32)
    sumsq = jnp.sum(arrived_wide * arrived_wide, axis=1)
    scaled = (arrived_wide * norm_gain[None, :]).astype(jnp.bfloat16)
    gate_part = jnp.dot(scaled, w_gate[0], preferred_element_type=jnp.float32)
    up_part = jnp.dot(scaled, w_up[0], preferred_element_type=jnp.float32)
    gate_part, up_part, sumsq = lax.psum((gate_part, up_part, sumsq), "ctx")
    inverse = lax.rsqrt(sumsq / D + epsilon)[:, None]
    active = (jax.nn.silu(inverse * gate_part) * (inverse * up_part)).astype(jnp.bfloat16)
    produced = jnp.dot(active, w_down[0], preferred_element_type=jnp.float32).astype(jnp.bfloat16)
    returned = lax.all_to_all(
        produced.reshape(experts, capacity, width_dev),
        ("row", "exp"),
        split_axis=0,
        concat_axis=0,
        tiled=True,
    )
    weighted = jnp.sum(gate_weights[:, :, None] * onehot.astype(jnp.float32), axis=1)
    combine = weighted[:, :, None] * slot_match.astype(jnp.float32)
    mixture = jnp.einsum(
        "bxs,xsd->bd", combine, returned.astype(jnp.float32), precision=lax.Precision.HIGHEST
    )
    return (hidden.astype(jnp.float32) + mixture).astype(jnp.bfloat16)


F32 = jnp.float32
BF16 = jnp.bfloat16
MESH = pl.DeviceIdType.MESH
DEAD = -1e30
FLOOR = -1e29
RATE = QK_HEAD ** (-0.5) * math.log2(math.e)


def iota(shape, dim):
    return lax.broadcasted_iota(jnp.int32, shape, dim)


def mm(a, b):
    return jnp.dot(a, b, preferred_element_type=F32)


def onehot(cond):
    return jnp.where(cond, 1.0, 0.0).astype(BF16)


def routing(expert, ids, gates, rows, picks):
    weights, slots = [], []
    before = jnp.zeros(expert.shape, jnp.int32)
    for b in range(rows):
        weight = jnp.zeros(expert.shape, F32)
        for k in range(picks):
            weight = jnp.where(expert == ids[b, k], gates[b, k], weight)
        weights.append(weight)
        slots.append(before)
        before = before + jnp.where(weight > 0.0, 1, 0)
    return weights, slots


def layer_kernel(
    queries, cache_hbm, lengths, wv_hbm, wo_hbm, stream, gain, ids, gates, wg_hbm, wu_hbm, wd_hbm,
    out,
    cache, wv, wo, wg, wu, wd,
    scores, msg, xr, ats, ar, vals, osend0, oown0, orecv0, rsend0, rrecv0, osend1, oown1, orecv1, rsend1, rrecv1, hid4, blocks,
    tsend, trecv, xsel, gusend, gurecv, sqsend, sqrecv, made, psend, precv, combine,
    cache_sem, w_sem, x_ss, x_rs, a_ss, a_rs, o_ss, o_rs, r_ss, r_rs, g_ss, g_rs, t_ss, t_rs,
    u_ss, u_rs, p_ss, p_rs,
):
    rows, _, heads = queries.shape
    block = cache_hbm.shape[2]
    latent = wv_hbm.shape[1]
    n_exp = lax.axis_size("exp")
    devs = lax.axis_size("row") * n_exp
    picks = ids.shape[1]
    per_dev = wv_hbm.shape[0]
    width = stream.shape[1]
    part, w0 = width // 4, 512
    w1 = part - w0
    c, r, e = lax.axis_index("ctx"), lax.axis_index("row"), lax.axis_index("exp")
    g = r * n_exp + e
    z, y = e // 2, lax.rem(e, 2)
    half_heads = heads // 2

    def remote(src, dst, ss, rs, ctx=None, row=None, exp=None):
        where = {
            "ctx": c if ctx is None else ctx,
            "row": r if row is None else row,
            "exp": e if exp is None else exp,
        }
        return pltpu.make_async_remote_copy(
            src_ref=src, dst_ref=dst, send_sem=ss, recv_sem=rs, device_id=where, device_id_type=MESH
        )

    def each(low, high, body, unroll=True):
        def step(i, carry):
            body(i)
            return carry

        lax.fori_loop(low, high, step, 0, unroll=unroll)

    def cache_copy(b):
        slot = lax.rem(b, 2)
        return pltpu.make_async_copy(cache_hbm.at[b], cache.at[slot], cache_sem.at[slot])

    def half_of(i):
        side = (1 - c) if i == 0 else c
        return wo_hbm.at[:, pl.ds(pl.multiple_of(side * width, 128), width)]

    weight_copies = [
        pltpu.make_async_copy(wv_hbm, wv, w_sem.at[0]),
        pltpu.make_async_copy(half_of(0), wo.at[0], w_sem.at[1]),
        pltpu.make_async_copy(half_of(1), wo.at[1], w_sem.at[2]),
        pltpu.make_async_copy(wg_hbm.at[0], wg, w_sem.at[3]),
        pltpu.make_async_copy(wu_hbm.at[0], wu, w_sem.at[4]),
        pltpu.make_async_copy(wd_hbm.at[0], wd, w_sem.at[5]),
    ]

    cache_copy(0).start()
    cache_copy(1).start()

    barrier = pltpu.get_barrier_semaphore()
    pl.semaphore_signal(
        barrier, inc=1, device_id={"ctx": 1 - c, "row": r, "exp": e}, device_id_type=MESH
    )

    def greet(d):
        to = lax.rem(g + d, devs)
        pl.semaphore_signal(
            barrier, inc=1, device_id={"ctx": c, "row": to // n_exp, "exp": lax.rem(to, n_exp)},
            device_id_type=MESH,
        )

    each(1, devs, greet)

    pl.semaphore_wait(barrier, devs)

    def tile_copy(d, back=False):
        to = lax.rem(g + d, devs)
        return remote(
            tsend.at[to], trecv.at[to if back else g], t_ss.at[to], t_rs.at[to if back else g],
            row=to // n_exp, exp=lax.rem(to, n_exp),
        )

    def swap(b):
        return remote(msg.at[b, 1 - c], xr.at[b], x_ss.at[b], x_rs.at[b], ctx=1 - c)

    def att_copy(b, d, back=False):
        to = lax.rem(e + d, n_exp)
        return remote(
            ats.at[b, to], ar.at[to if back else e, b],
            a_ss.at[b, to], a_rs.at[b, to if back else e], exp=to,
        )

    def attend(b):
        slot = lax.rem(b, 2)
        cache_copy(b).wait()
        query = queries[b].T
        live = lengths[b] - c * block
        step = 1024
        tops = []
        for t in range(block // step):
            span = slice(t * step, (t + 1) * step)
            s = mm(query, cache[slot, :, span])
            s = jnp.where(iota(s.shape, 1) + t * step < live, s, DEAD)
            scores[:, span] = s
            tops.append(jnp.max(s, axis=1, keepdims=True))
        top = tops[0]
        for other in tops[1:]:
            top = jnp.maximum(top, other)
        top = jnp.maximum(top, FLOOR).astype(BF16).astype(F32)
        total = jnp.zeros_like(top)
        acc = jnp.zeros((latent, heads), F32)
        for t in range(block // step):
            span = slice(t * step, (t + 1) * step)
            p = jnp.exp2((scores[:, span] - top) * RATE)
            total += jnp.sum(p, axis=1, keepdims=True)
            acc += lax.dot_general(
                cache[slot, 0:latent, span], p.astype(BF16), (((1,), (1,)), ((), ())),
                preferred_element_type=F32,
            )
        lane = iota((heads, 128), 1)
        rest = total - total.astype(BF16).astype(F32)
        aux = jnp.where(lane == 0, top, jnp.where(lane == 1, total, jnp.where(lane == 2, rest, 0.0)))
        acc, aux = acc.T.astype(BF16), aux.astype(BF16)
        for side in range(2):
            mine = slice(side * half_heads, (side + 1) * half_heads)
            msg[b, side, :, 0:latent] = acc[mine]
            msg[b, side, :, latent : latent + 128] = aux[mine]
        swap(b).start()

    def merge(b):
        swap(b).wait_recv()
        one, two = msg[b, c].astype(F32), xr[b].astype(F32)

        def aux_of(m):
            return m[:, latent : latent + 1], m[:, latent + 1 : latent + 2] + m[:, latent + 2 : latent + 3]

        (top1, sum1), (top2, sum2) = aux_of(one), aux_of(two)
        top = jnp.maximum(top1, top2)
        f1, f2 = jnp.exp2((top1 - top) * RATE), jnp.exp2((top2 - top) * RATE)
        inv = 1.0 / (f1 * sum1 + f2 * sum2)
        att = (f1 * inv) * one[:, 0:latent] + (f2 * inv) * two[:, 0:latent]
        att = att.reshape(n_exp, per_dev, latent)
        half = latent // 2
        ats[b] = jnp.concatenate([att[:, :, 0:half], att[:, :, half:]], axis=1).astype(BF16)
        ar[e, b] = ats[b, e]
        each(1, n_exp, lambda d: att_copy(b, d).start())

    def row_step(b):
        attend(b)

        @pl.when(b < rows - 2)
        def _():
            cache_copy(b + 2).start()

        @pl.when(b == 1)
        def _():
            merge(0)
            for w in weight_copies[0:3]:
                w.start()

        @pl.when(b == 2)
        def _():
            merge(1)
            for w in weight_copies[3:5]:
                w.start()

        @pl.when(b == 3)
        def _():
            merge(2)
            weight_copies[5].start()

    each(0, rows, row_step, False)
    merge(3)

    shape = (devs, 8, 128)
    expert, sub, lane = iota(shape, 0), iota(shape, 1), iota(shape, 2)
    weights, slots = routing(expert, ids, gates, rows, picks)
    tile = jnp.zeros(shape, F32)
    for b in range(rows):
        here = ((lane & 3) == b) & (sub == 2 * lax.rem(g, 4) + slots[b])
        tile = jnp.where(here, weights[b], tile)
    tsend[...] = tile
    trecv[g] = tsend[g]
    each(1, devs, lambda d: tile_copy(d).start())

    weight_copies[0].wait()
    for b in range(rows):
        each(1, n_exp, lambda d: att_copy(b, d, True).wait_recv())
    n_rows = n_exp * rows
    x = ar[...].astype(F32).reshape(n_rows, 2, per_dev, latent // 2)
    x = jnp.concatenate([x[:, 0], x[:, 1]], axis=2).reshape(n_rows * per_dev, latent).astype(BF16)
    for h in range(per_dev):
        v = mm(x, wv[h])
        v = jnp.where((iota(v.shape, 0) & (per_dev - 1)) == h, v, 0.0)
        v = jnp.sum(v.reshape(n_rows, per_dev, v.shape[1]), axis=1)
        vals[:, h * v.shape[1] : (h + 1) * v.shape[1]] = v.astype(BF16)

    def cuts(k):
        return slice(k * w0, (k + 1) * w0), slice(4 * w0 + k * w1, 4 * w0 + (k + 1) * w1)

    osend, oown, orecv, rsend, rrecv = (osend0, osend1), (oown0, oown1), (orecv0, orecv1), (rsend0, rsend1), (rrecv0, rrecv1)

    def term_copy(q):
        return remote(osend[q], orecv[q], o_ss.at[q], o_rs.at[q], ctx=1 - c)

    def red_copy(q, d, back=False):
        to = lax.rem(e + d, n_exp)
        return remote(
            rsend[q].at[to], rrecv[q].at[to if back else e],
            r_ss.at[q, to], r_rs.at[q, to if back else e], exp=to,
        )

    weight_copies[1].wait()
    for q in range(2):
        for k in range(4):
            osend[q][k] = mm(vals[...], wo[0, :, cuts(k)[q]]).astype(BF16)
        term_copy(q).start()
    weight_copies[2].wait()
    shape = (4 * n_rows, 4 * n_rows)
    i, j = iota(shape, 0), iota(shape, 1)
    spread = onehot(j == (((i & 15) >> 2) * n_rows + (i >> 4) * 4 + (i & 3)))
    for q in range(2):
        for k in range(4):
            oown[q][k] = mm(vals[...], wo[1, :, cuts(k)[q]])
        term_copy(q).wait_recv()
        both = oown[q][...] + orecv[q][...].astype(F32)
        both = both.reshape(4 * n_rows, both.shape[2]).astype(BF16)
        rsend[q][...] = mm(spread, both).astype(BF16).reshape(rsend[q].shape)
        rrecv[q][e] = rsend[q][e]
        each(1, n_exp, lambda d: red_copy(q, d).start())
    wide = stream[...].astype(F32)
    base = jnp.concatenate(
        [jnp.concatenate([wide[:, cut] for cut in cuts(k)], axis=1) for k in range(4)], axis=0
    )
    for q in range(2):
        each(1, n_exp, lambda d: red_copy(q, d, True).wait_recv())
    attn = jnp.concatenate([jnp.sum(rrecv[q][...].astype(F32), axis=0) for q in range(2)], axis=1)
    hidden = (base + attn).astype(BF16)
    blocks[g] = hidden

    def pass_on(number, sem, row=None, exp=None):
        return remote(blocks.at[number], blocks.at[number], g_ss.at[sem], g_rs.at[number], row=row, exp=exp)

    def arrive(number):
        remote(blocks.at[number], blocks.at[number], g_ss.at[15], g_rs.at[number], row=1 - r).wait_recv()

    nz = n_exp // 2
    e_y = z * 2 + (1 - y)

    def own_z(d):
        pass_on(g, d - 1, exp=lax.rem(z + d, nz) * 2 + y).start()

    pass_on(g, 3, exp=e_y).start()
    each(1, nz, own_z)
    pass_on(g, 4, row=1 - r).start()

    def relay_z(d):
        number = r * n_exp + lax.rem(z + d, nz) * 2 + y
        arrive(number)
        pass_on(number, 4 + d, exp=e_y).start()
        pass_on(number, 7 + d, row=1 - r).start()

    each(1, nz, relay_z)

    def relay_y(d):
        number = r * n_exp + lax.rem(z + d, nz) * 2 + (1 - y)
        arrive(number)
        pass_on(number, 11 + d, row=1 - r).start()

    each(0, nz, relay_y)
    hw = hidden.astype(F32)
    for k in range(4):
        for cut, lanes in zip(cuts(k), (slice(0, w0), slice(w0, part))):
            hid4[:, cut] = hw[4 * k : 4 * k + 4, lanes]
    each(1, devs, lambda d: tile_copy(d, True).wait_recv())
    slots_n = 2 * devs
    used = jnp.sum(trecv[...].reshape(devs // 4, 4, 8, 128), axis=1).reshape(slots_n, 128)
    used = jnp.concatenate([used, used], axis=1)
    line, col = iota(used.shape, 0), iota(used.shape, 1)
    used = (used > 0.0) & ((col >> 4) == (line >> 1))
    each(0, n_exp, lambda j: arrive((1 - r) * n_exp + j))

    sumsq = jnp.zeros((slots_n, 1), F32)
    scale = gain[...].reshape(1, width)
    flat = blocks[...].reshape(devs * 16, part)
    for k in range(4):
        xk = mm(onehot(used & (((col & 15) >> 2) == k)), flat)
        sumsq += jnp.sum(xk * xk, axis=1, keepdims=True)
        for cut, lanes in zip(cuts(k), (slice(0, w0), slice(w0, part))):
            xsel[:, cut] = (xk[:, lanes] * scale[:, cut]).astype(BF16)
    sqsend[...] = jnp.broadcast_to(sumsq, sqsend.shape)
    sq = remote(sqsend, sqrecv, u_ss.at[2], u_rs.at[2], ctx=1 - c)
    sq.start()
    weight_copies[3].wait()
    weight_copies[4].wait()
    ffe = wg.shape[1]
    hf = ffe // 2

    def gu_copy(f):
        return remote(gusend.at[f], gurecv.at[f], u_ss.at[f], u_rs.at[f], ctx=1 - c)

    own = []
    for f in range(2):
        cut = slice(f * hf, (f + 1) * hf)
        gate, up = mm(xsel[...], wg[:, cut]), mm(xsel[...], wu[:, cut])
        own.append((gate, up))
        gusend[f, 0:slots_n] = gate.astype(BF16)
        gusend[f, slots_n : 2 * slots_n] = up.astype(BF16)
        gu_copy(f).start()
    sq.wait_recv()
    inverse = lax.rsqrt((sumsq + sqrecv[:, 0:1]) / D + epsilon)
    active = []
    for f in range(2):
        gu_copy(f).wait_recv()
        gate = inverse * (own[f][0] + gurecv[f, 0:slots_n].astype(F32))
        up = inverse * (own[f][1] + gurecv[f, slots_n : 2 * slots_n].astype(F32))
        active.append((gate / (1.0 + jnp.exp(-gate)) * up).astype(BF16))
    active = jnp.concatenate(active, axis=1)
    weight_copies[5].wait()
    for k in range(7):
        made[k * slots_n : (k + 1) * slots_n, :] = mm(active, wd[:, k * 512 : (k + 1) * 512]).astype(BF16)
    shape = (devs * 16, 7 * slots_n)
    i, j = iota(shape, 0), iota(shape, 1)
    spread = onehot(j == (((i & 15) >> 1) * slots_n + (i >> 4) * 2 + (i & 1)))
    psend[...] = mm(spread, made[...]).astype(BF16).reshape(devs, 16, 512)
    precv[g] = psend[g]

    def back_copy(d, back=False):
        to = lax.rem(g + d, devs)
        return remote(
            psend.at[to], precv.at[to if back else g], p_ss.at[to], p_rs.at[to if back else g],
            row=to // n_exp, exp=lax.rem(to, n_exp),
        )

    each(1, devs, lambda d: back_copy(d).start())

    shape = (32, devs * 16)
    line, col = iota(shape, 0), iota(shape, 1)
    weights, slots = routing(col >> 4, ids, gates, rows, picks)
    comb = jnp.zeros(shape, F32)
    for b in range(rows):
        here = ((line & 3) == b) & ((line >> 2) == ((col & 15) >> 1)) & ((col & 1) == slots[b])
        comb = jnp.where(here, weights[b], comb)
    high = comb.astype(BF16)
    combine[0:32, :] = high
    combine[32:64, :] = (comb - high.astype(F32)).astype(BF16)

    each(1, devs, lambda d: tile_copy(d).wait_send())
    each(0, rows, lambda b: swap(b).wait_send())
    for b in range(rows):
        each(1, n_exp, lambda d: att_copy(b, d).wait_send())
    for q in range(2):
        term_copy(q).wait_send()
        each(1, n_exp, lambda d: red_copy(q, d).wait_send())
    each(0, 15, lambda i: pass_on(g, i, row=1 - r).wait_send())
    sq.wait_send()
    for f in range(2):
        gu_copy(f).wait_send()

    each(1, devs, lambda d: back_copy(d, True).wait_recv())
    mix = mm(combine[...], precv[...].reshape(devs * 16, 512))
    mix = mix[0:32] + mix[32:64]
    for k in range(7):
        cut = slice(k * 512, (k + 1) * 512)
        out[:, cut] = (hid4[:, cut] + mix[4 * k : 4 * k + 4]).astype(BF16)
    each(1, devs, lambda d: back_copy(d).wait_send())


def fused(
    queries, latent_cache, lengths, w_value, w_out, stream, norm_gain, expert_ids, gate_weights,
    w_gate, w_up, w_down,
):
    rows, heads, qk = queries.shape
    block = latent_cache.shape[1]
    per_dev, latent, v_head = w_value.shape
    width = stream.shape[1]
    n_exp = lax.axis_size("exp")
    devs = n_exp * lax.axis_size("row")
    depth, ffe = w_out.shape[0], w_gate.shape[2]
    part, n_rows, slots_n = width // 4, n_exp * rows, 2 * devs
    vmem, smem, anyw = (pl.BlockSpec(memory_space=s) for s in (pltpu.VMEM, pltpu.SMEM, pl.ANY))
    dma = pltpu.SemaphoreType.DMA
    scratch = [
        pltpu.VMEM((2, qk, block), BF16),
        pltpu.VMEM(w_value.shape, BF16),
        pltpu.VMEM((2, depth, width), BF16),
        pltpu.VMEM((width, ffe), BF16),
        pltpu.VMEM((width, ffe), BF16),
        pltpu.VMEM((ffe, width), BF16),
        pltpu.VMEM((heads, block), F32),
        pltpu.VMEM((rows, 2, heads // 2, latent + 128), BF16),
        pltpu.VMEM((rows, heads // 2, latent + 128), BF16),
        pltpu.VMEM((rows, n_exp, 16, latent // 2), BF16),
        pltpu.VMEM((n_exp, rows, 16, latent // 2), BF16),
        pltpu.VMEM((n_rows, depth), BF16),
        *(
            buffer
            for piece in (512, part - 512)
            for buffer in (
                pltpu.VMEM((4, n_rows, piece), BF16),
                pltpu.VMEM((4, n_rows, piece), F32),
                pltpu.VMEM((4, n_rows, piece), BF16),
                pltpu.VMEM((n_exp, 16, piece), BF16),
                pltpu.VMEM((n_exp, 16, piece), BF16),
            )
        ),
        pltpu.VMEM((rows, width), F32),
        pltpu.VMEM((devs, 16, part), BF16),
        pltpu.VMEM((devs, 8, 128), F32),
        pltpu.VMEM((devs, 8, 128), F32),
        pltpu.VMEM((slots_n, width), BF16),
        pltpu.VMEM((2, 2 * slots_n, ffe // 2), BF16),
        pltpu.VMEM((2, 2 * slots_n, ffe // 2), BF16),
        pltpu.VMEM((slots_n, 128), F32),
        pltpu.VMEM((slots_n, 128), F32),
        pltpu.VMEM((7 * slots_n, 512), BF16),
        pltpu.VMEM((devs, 16, 512), BF16),
        pltpu.VMEM((devs, 16, 512), BF16),
        pltpu.VMEM((64, devs * 16), BF16),
    ] + [
        dma(s)
        for s in (
            (2,), (6,), (rows,), (rows,), (rows, n_exp), (rows, n_exp), (2,), (2,), (2, n_exp), (2, n_exp),
            (16,), (devs,), (devs,), (devs,), (3,), (3,), (devs,), (devs,),
        )
    ]
    return pl.pallas_call(
        layer_kernel,
        out_shape=jax.ShapeDtypeStruct((rows, width), BF16),
        in_specs=[vmem, anyw, smem, anyw, anyw, vmem, vmem, smem, smem, anyw, anyw, anyw],
        out_specs=vmem,
        scratch_shapes=scratch,
        compiler_params=pltpu.CompilerParams(
            collective_id=0, has_side_effects=True, vmem_limit_bytes=60 * 1024 * 1024
        ),
    )(
        jnp.swapaxes(queries, 1, 2), jnp.swapaxes(latent_cache, 1, 2), lengths, w_value, w_out, stream,
        norm_gain, expert_ids, gate_weights, w_gate, w_up, w_down,
    )


def solution(mesh):
    placed = (
        P(("row", "exp"), None, None),
        P(("row", "exp"), "ctx", None),
        P(("row", "exp")),
        P(("ctx", "exp"), None, None),
        P(("ctx", "exp"), None),
        P(("row", "exp"), "ctx"),
        P("ctx"),
        P(("row", "exp"), None),
        P(("row", "exp"), None),
        P(("row", "exp"), "ctx", None),
        P(("row", "exp"), "ctx", None),
        P(("row", "exp"), None, "ctx"),
    )
    sizes = tuple(mesh.shape[axis] for axis in ("ctx", "row", "exp"))
    body = fused if sizes == (2, 2, 8) else on_device
    return jax.shard_map(
        body, mesh=mesh, in_specs=placed, out_specs=P(("row", "exp"), "ctx"), check_vma=False
    )
```

```python
import math

import jax
import jax.numpy as jnp
from jax import lax
from jax.experimental import pallas as pl
from jax.experimental.pallas import tpu as pltpu
from jax.sharding import PartitionSpec as P

D = 7168
QK_HEAD = 192


epsilon = 1e-06


def merge_blocks(outputs, maxima, totals):
    top_value = jnp.max(maxima, axis=0)
    factor = jnp.exp(maxima - top_value[None])
    numer = jnp.sum(factor[..., None] * outputs, axis=0)
    denom = jnp.sum(factor * totals, axis=0)
    return (numer / denom[..., None]).astype(jnp.bfloat16)


def on_device(
    queries,
    latent_cache,
    lengths,
    w_value,
    w_out,
    stream,
    norm_gain,
    expert_ids,
    gate_weights,
    w_gate,
    w_up,
    w_down,
):
    n_ctx = lax.axis_size("ctx")
    n_row = lax.axis_size("row")
    n_exp = lax.axis_size("exp")
    groups = queries.shape[0]
    block = latent_cache.shape[1]
    per_dev = w_value.shape[0]
    latent = w_value.shape[1]
    scores = jnp.einsum(
        "bhw,btw->bht", queries, latent_cache, preferred_element_type=jnp.float32
    ) * QK_HEAD ** (-0.5)
    position = lax.axis_index("ctx") * block + jnp.arange(block, dtype=jnp.int32)
    live = (position[None, :] < lengths[:, None])[:, None, :]
    block_max = jnp.max(jnp.where(live, scores, -jnp.inf), axis=2)
    shift_by = jnp.where(jnp.isfinite(block_max), block_max, 0.0)
    weights = jnp.where(live, jnp.exp(scores - shift_by[..., None]), 0.0)
    totals = jnp.sum(weights, axis=2)
    latent_out = jnp.einsum(
        "bht,btl->bhl",
        weights.astype(jnp.bfloat16),
        latent_cache[:, :, :latent],
        preferred_element_type=jnp.float32,
    )
    outputs, maxima, sums = (
        lax.all_to_all(
            latent_out.reshape(1, groups, n_ctx * n_exp, per_dev, latent),
            ("ctx", "exp"),
            split_axis=2,
            concat_axis=0,
            tiled=True,
        ),
        lax.all_to_all(
            block_max.reshape(1, groups, n_ctx * n_exp, per_dev),
            ("ctx", "exp"),
            split_axis=2,
            concat_axis=0,
            tiled=True,
        ),
        lax.all_to_all(
            totals.reshape(1, groups, n_ctx * n_exp, per_dev),
            ("ctx", "exp"),
            split_axis=2,
            concat_axis=0,
            tiled=True,
        ),
    )
    gathered_rows = n_exp * groups
    attended = merge_blocks(
        outputs.reshape(n_ctx, gathered_rows, per_dev, latent),
        maxima.reshape(n_ctx, gathered_rows, per_dev),
        sums.reshape(n_ctx, gathered_rows, per_dev),
    )
    values = jnp.einsum("nhl,hlv->nhv", attended, w_value, preferred_element_type=jnp.float32)
    values = values.astype(jnp.bfloat16).reshape(gathered_rows, -1)
    split_out = w_out.reshape(w_out.shape[0], n_ctx, -1)
    term_rows = jnp.einsum(
        "nk,kcd->cnd", values, split_out, preferred_element_type=jnp.float32
    ).reshape(n_ctx * gathered_rows, -1)
    attn_out = lax.psum_scatter(term_rows, ("ctx", "exp"), scatter_dimension=0, tiled=True)
    hidden = lax.optimization_barrier((stream.astype(jnp.float32) + attn_out).astype(jnp.bfloat16))
    experts = n_row * n_exp
    picks = expert_ids.shape[1]
    capacity = max(2, (groups * picks + experts - 1) // experts)
    expert_range = jnp.arange(experts, dtype=jnp.int32)
    onehot = expert_ids[:, :, None] == expert_range[None, None, :]
    named = jnp.sum(onehot.astype(jnp.int32), axis=1)
    slot_of = jnp.cumsum(named, axis=0) - named
    slot_match = slot_of[:, :, None] == jnp.arange(capacity, dtype=jnp.int32)[None, None, :]
    placed = (named[:, :, None] == 1) & slot_match
    outgoing = jnp.einsum(
        "bxs,bd->xsd", placed.astype(jnp.bfloat16), hidden, preferred_element_type=jnp.float32
    ).astype(jnp.bfloat16)
    width_dev = outgoing.shape[2]
    arrived = lax.all_to_all(outgoing, ("row", "exp"), split_axis=0, concat_axis=0, tiled=True)
    arrived = arrived.reshape(experts * capacity, width_dev)
    arrived_wide = arrived.astype(jnp.float32)
    sumsq = jnp.sum(arrived_wide * arrived_wide, axis=1)
    scaled = (arrived_wide * norm_gain[None, :]).astype(jnp.bfloat16)
    gate_part = jnp.dot(scaled, w_gate[0], preferred_element_type=jnp.float32)
    up_part = jnp.dot(scaled, w_up[0], preferred_element_type=jnp.float32)
    gate_part, up_part, sumsq = lax.psum((gate_part, up_part, sumsq), "ctx")
    inverse = lax.rsqrt(sumsq / D + epsilon)[:, None]
    active = (jax.nn.silu(inverse * gate_part) * (inverse * up_part)).astype(jnp.bfloat16)
    produced = jnp.dot(active, w_down[0], preferred_element_type=jnp.float32).astype(jnp.bfloat16)
    returned = lax.all_to_all(
        produced.reshape(experts, capacity, width_dev),
        ("row", "exp"),
        split_axis=0,
        concat_axis=0,
        tiled=True,
    )
    weighted = jnp.sum(gate_weights[:, :, None] * onehot.astype(jnp.float32), axis=1)
    combine = weighted[:, :, None] * slot_match.astype(jnp.float32)
    mixture = jnp.einsum(
        "bxs,xsd->bd", combine, returned.astype(jnp.float32), precision=lax.Precision.HIGHEST
    )
    return (hidden.astype(jnp.float32) + mixture).astype(jnp.bfloat16)


F32 = jnp.float32
BF16 = jnp.bfloat16
MESH = pl.DeviceIdType.MESH
DEAD = -1e30
FLOOR = -1e29
RATE = QK_HEAD ** (-0.5) * math.log2(math.e)


def iota(shape, dim):
    return lax.broadcasted_iota(jnp.int32, shape, dim)


def mm(a, b):
    return jnp.dot(a, b, preferred_element_type=F32)


def onehot(cond):
    return jnp.where(cond, 1.0, 0.0).astype(BF16)


def routing(expert, ids, gates, rows, picks):
    weights, slots = [], []
    before = jnp.zeros(expert.shape, jnp.int32)
    for b in range(rows):
        weight = jnp.zeros(expert.shape, F32)
        for k in range(picks):
            weight = jnp.where(expert == ids[b, k], gates[b, k], weight)
        weights.append(weight)
        slots.append(before)
        before = before + jnp.where(weight > 0.0, 1, 0)
    return weights, slots


def layer_kernel(
    queries, cache_hbm, lengths, wv_hbm, wo_hbm, stream, gain, ids, gates, wg_hbm, wu_hbm, wd_hbm,
    out,
    cache, wv, wo, wg, wu, wd,
    scores, msg, xr, ats, ar, vals, osend0, oown0, orecv0, rsend0, rrecv0, osend1, oown1, orecv1, rsend1, rrecv1, hid4, blocks,
    tsend, trecv, xsel, gusend, gurecv, sqsend, sqrecv, made, psend, precv, combine,
    cache_sem, w_sem, x_ss, x_rs, a_ss, a_rs, o_ss, o_rs, r_ss, r_rs, g_ss, g_rs, t_ss, t_rs,
    u_ss, u_rs, p_ss, p_rs,
):
    rows, _, heads = queries.shape
    block = cache_hbm.shape[2]
    latent = wv_hbm.shape[1]
    n_exp = lax.axis_size("exp")
    devs = lax.axis_size("row") * n_exp
    picks = ids.shape[1]
    per_dev = wv_hbm.shape[0]
    width = stream.shape[1]
    part, w0 = width // 4, 512
    w1 = part - w0
    c, r, e = lax.axis_index("ctx"), lax.axis_index("row"), lax.axis_index("exp")
    g = r * n_exp + e
    z, y = e // 2, lax.rem(e, 2)
    half_heads = heads // 2

    def remote(src, dst, ss, rs, ctx=None, row=None, exp=None):
        where = {
            "ctx": c if ctx is None else ctx,
            "row": r if row is None else row,
            "exp": e if exp is None else exp,
        }
        return pltpu.make_async_remote_copy(
            src_ref=src, dst_ref=dst, send_sem=ss, recv_sem=rs, device_id=where, device_id_type=MESH
        )

    def each(low, high, body, unroll=True):
        def step(i, carry):
            body(i)
            return carry

        lax.fori_loop(low, high, step, 0, unroll=unroll)

    class Pieces:
        def __init__(self, copies):
            self.copies = copies

        def start(self):
            for copy in self.copies:
                copy.start()

        def wait(self):
            for copy in self.copies:
                copy.wait()

    def cache_copy(b):
        slot = lax.rem(b, 2)
        step = cache_hbm.shape[1] // 4
        return Pieces(
            [
                pltpu.make_async_copy(
                    cache_hbm.at[b, i * step : (i + 1) * step],
                    cache.at[slot, i * step : (i + 1) * step],
                    cache_sem.at[slot, i],
                )
                for i in range(4)
            ]
        )

    def in_pieces(src, dst, number):
        step = dst.shape[0] // 4
        return Pieces(
            [
                pltpu.make_async_copy(
                    src.at[i * step : (i + 1) * step], dst.at[i * step : (i + 1) * step], w_sem.at[number, i]
                )
                for i in range(4)
            ]
        )

    def half_of(i):
        side = (1 - c) if i == 0 else c
        return wo_hbm.at[:, pl.ds(pl.multiple_of(side * width, 128), width)]

    weight_copies = [
        in_pieces(wv_hbm, wv, 0),
        in_pieces(half_of(0), wo.at[0], 1),
        in_pieces(half_of(1), wo.at[1], 2),
        in_pieces(wg_hbm.at[0], wg, 3),
        in_pieces(wu_hbm.at[0], wu, 4),
        in_pieces(wd_hbm.at[0], wd, 5),
    ]

    cache_copy(0).start()
    cache_copy(1).start()

    barrier = pltpu.get_barrier_semaphore()
    pl.semaphore_signal(
        barrier, inc=1, device_id={"ctx": 1 - c, "row": r, "exp": e}, device_id_type=MESH
    )

    def greet(d):
        to = lax.rem(g + d, devs)
        pl.semaphore_signal(
            barrier, inc=1, device_id={"ctx": c, "row": to // n_exp, "exp": lax.rem(to, n_exp)},
            device_id_type=MESH,
        )

    each(1, devs, greet)

    pl.semaphore_wait(barrier, devs)

    def tile_copy(d, back=False):
        to = lax.rem(g + d, devs)
        return remote(
            tsend.at[to], trecv.at[to if back else g], t_ss.at[to], t_rs.at[to if back else g],
            row=to // n_exp, exp=lax.rem(to, n_exp),
        )

    def swap(b):
        return remote(msg.at[b, 1 - c], xr.at[b], x_ss.at[b], x_rs.at[b], ctx=1 - c)

    def att_copy(b, d, back=False):
        to = lax.rem(e + d, n_exp)
        return remote(
            ats.at[b, to], ar.at[to if back else e, b],
            a_ss.at[b, to], a_rs.at[b, to if back else e], exp=to,
        )

    def attend(b):
        slot = lax.rem(b, 2)
        cache_copy(b).wait()
        query = queries[b].T
        live = lengths[b] - c * block
        step = 1024
        tops = []
        for t in range(block // step):
            span = slice(t * step, (t + 1) * step)
            s = mm(query, cache[slot, :, span])
            s = jnp.where(iota(s.shape, 1) + t * step < live, s, DEAD)
            scores[:, span] = s
            tops.append(jnp.max(s, axis=1, keepdims=True))
        top = tops[0]
        for other in tops[1:]:
            top = jnp.maximum(top, other)
        top = jnp.maximum(top, FLOOR).astype(BF16).astype(F32)
        total = jnp.zeros_like(top)
        acc = jnp.zeros((latent, heads), F32)
        for t in range(block // step):
            span = slice(t * step, (t + 1) * step)
            p = jnp.exp2((scores[:, span] - top) * RATE)
            total += jnp.sum(p, axis=1, keepdims=True)
            acc += lax.dot_general(
                cache[slot, 0:latent, span], p.astype(BF16), (((1,), (1,)), ((), ())),
                preferred_element_type=F32,
            )
        lane = iota((heads, 128), 1)
        rest = total - total.astype(BF16).astype(F32)
        aux = jnp.where(lane == 0, top, jnp.where(lane == 1, total, jnp.where(lane == 2, rest, 0.0)))
        acc, aux = acc.T.astype(BF16), aux.astype(BF16)
        for side in range(2):
            mine = slice(side * half_heads, (side + 1) * half_heads)
            msg[b, side, :, 0:latent] = acc[mine]
            msg[b, side, :, latent : latent + 128] = aux[mine]
        swap(b).start()

    def merge(b):
        swap(b).wait_recv()
        one, two = msg[b, c].astype(F32), xr[b].astype(F32)

        def aux_of(m):
            return m[:, latent : latent + 1], m[:, latent + 1 : latent + 2] + m[:, latent + 2 : latent + 3]

        (top1, sum1), (top2, sum2) = aux_of(one), aux_of(two)
        top = jnp.maximum(top1, top2)
        f1, f2 = jnp.exp2((top1 - top) * RATE), jnp.exp2((top2 - top) * RATE)
        inv = 1.0 / (f1 * sum1 + f2 * sum2)
        att = (f1 * inv) * one[:, 0:latent] + (f2 * inv) * two[:, 0:latent]
        att = att.reshape(n_exp, per_dev, latent)
        half = latent // 2
        ats[b] = jnp.concatenate([att[:, :, 0:half], att[:, :, half:]], axis=1).astype(BF16)
        ar[e, b] = ats[b, e]
        each(1, n_exp, lambda d: att_copy(b, d).start())

    def row_step(b):
        attend(b)

        @pl.when(b < rows - 2)
        def _():
            cache_copy(b + 2).start()

        @pl.when(b == 1)
        def _():
            merge(0)
            for w in weight_copies[0:3]:
                w.start()

        @pl.when(b == 2)
        def _():
            merge(1)
            for w in weight_copies[3:5]:
                w.start()

        @pl.when(b == 3)
        def _():
            merge(2)
            weight_copies[5].start()

    each(0, rows, row_step, False)
    merge(3)

    shape = (devs, 8, 128)
    expert, sub, lane = iota(shape, 0), iota(shape, 1), iota(shape, 2)
    weights, slots = routing(expert, ids, gates, rows, picks)
    tile = jnp.zeros(shape, F32)
    for b in range(rows):
        here = ((lane & 3) == b) & (sub == 2 * lax.rem(g, 4) + slots[b])
        tile = jnp.where(here, weights[b], tile)
    tsend[...] = tile
    trecv[g] = tsend[g]
    each(1, devs, lambda d: tile_copy(d).start())

    weight_copies[0].wait()
    for b in range(rows):
        each(1, n_exp, lambda d: att_copy(b, d, True).wait_recv())
    n_rows = n_exp * rows
    x = ar[...].astype(F32).reshape(n_rows, 2, per_dev, latent // 2)
    x = jnp.concatenate([x[:, 0], x[:, 1]], axis=2).reshape(n_rows * per_dev, latent).astype(BF16)
    for h in range(per_dev):
        v = mm(x, wv[h])
        v = jnp.where((iota(v.shape, 0) & (per_dev - 1)) == h, v, 0.0)
        v = jnp.sum(v.reshape(n_rows, per_dev, v.shape[1]), axis=1)
        vals[:, h * v.shape[1] : (h + 1) * v.shape[1]] = v.astype(BF16)

    def cuts(k):
        return slice(k * w0, (k + 1) * w0), slice(4 * w0 + k * w1, 4 * w0 + (k + 1) * w1)

    osend, oown, orecv, rsend, rrecv = (osend0, osend1), (oown0, oown1), (orecv0, orecv1), (rsend0, rsend1), (rrecv0, rrecv1)

    def term_copy(q):
        return remote(osend[q], orecv[q], o_ss.at[q], o_rs.at[q], ctx=1 - c)

    def red_copy(q, d, back=False):
        to = lax.rem(e + d, n_exp)
        return remote(
            rsend[q].at[to], rrecv[q].at[to if back else e],
            r_ss.at[q, to], r_rs.at[q, to if back else e], exp=to,
        )

    weight_copies[1].wait()
    for q in range(2):
        for k in range(4):
            osend[q][k] = mm(vals[...], wo[0, :, cuts(k)[q]]).astype(BF16)
        term_copy(q).start()
    weight_copies[2].wait()
    shape = (4 * n_rows, 4 * n_rows)
    i, j = iota(shape, 0), iota(shape, 1)
    spread = onehot(j == (((i & 15) >> 2) * n_rows + (i >> 4) * 4 + (i & 3)))
    for q in range(2):
        for k in range(4):
            oown[q][k] = mm(vals[...], wo[1, :, cuts(k)[q]])
        term_copy(q).wait_recv()
        both = oown[q][...] + orecv[q][...].astype(F32)
        both = both.reshape(4 * n_rows, both.shape[2]).astype(BF16)
        rsend[q][...] = mm(spread, both).astype(BF16).reshape(rsend[q].shape)
        rrecv[q][e] = rsend[q][e]
        each(1, n_exp, lambda d: red_copy(q, d).start())
    wide = stream[...].astype(F32)
    base = jnp.concatenate(
        [jnp.concatenate([wide[:, cut] for cut in cuts(k)], axis=1) for k in range(4)], axis=0
    )
    for q in range(2):
        each(1, n_exp, lambda d: red_copy(q, d, True).wait_recv())
    attn = jnp.concatenate([jnp.sum(rrecv[q][...].astype(F32), axis=0) for q in range(2)], axis=1)
    hidden = (base + attn).astype(BF16)
    blocks[g] = hidden

    def pass_on(number, sem, row=None, exp=None):
        return remote(blocks.at[number], blocks.at[number], g_ss.at[sem], g_rs.at[number], row=row, exp=exp)

    def arrive(number):
        remote(blocks.at[number], blocks.at[number], g_ss.at[15], g_rs.at[number], row=1 - r).wait_recv()

    nz = n_exp // 2
    e_y = z * 2 + (1 - y)

    def own_z(d):
        pass_on(g, d - 1, exp=lax.rem(z + d, nz) * 2 + y).start()

    pass_on(g, 3, exp=e_y).start()
    each(1, nz, own_z)
    pass_on(g, 4, row=1 - r).start()

    def relay_z(d):
        number = r * n_exp + lax.rem(z + d, nz) * 2 + y
        arrive(number)
        pass_on(number, 4 + d, exp=e_y).start()
        pass_on(number, 7 + d, row=1 - r).start()

    each(1, nz, relay_z)

    def relay_y(d):
        number = r * n_exp + lax.rem(z + d, nz) * 2 + (1 - y)
        arrive(number)
        pass_on(number, 11 + d, row=1 - r).start()

    each(0, nz, relay_y)
    hw = hidden.astype(F32)
    for k in range(4):
        for cut, lanes in zip(cuts(k), (slice(0, w0), slice(w0, part))):
            hid4[:, cut] = hw[4 * k : 4 * k + 4, lanes]
    each(1, devs, lambda d: tile_copy(d, True).wait_recv())
    slots_n = 2 * devs
    used = jnp.sum(trecv[...].reshape(devs // 4, 4, 8, 128), axis=1).reshape(slots_n, 128)
    used = jnp.concatenate([used, used], axis=1)
    line, col = iota(used.shape, 0), iota(used.shape, 1)
    used = (used > 0.0) & ((col >> 4) == (line >> 1))
    each(0, n_exp, lambda j: arrive((1 - r) * n_exp + j))

    sumsq = jnp.zeros((slots_n, 1), F32)
    scale = gain[...].reshape(1, width)
    flat = blocks[...].reshape(devs * 16, part)
    for k in range(4):
        xk = mm(onehot(used & (((col & 15) >> 2) == k)), flat)
        sumsq += jnp.sum(xk * xk, axis=1, keepdims=True)
        for cut, lanes in zip(cuts(k), (slice(0, w0), slice(w0, part))):
            xsel[:, cut] = (xk[:, lanes] * scale[:, cut]).astype(BF16)
    sqsend[...] = jnp.broadcast_to(sumsq, sqsend.shape)
    sq = remote(sqsend, sqrecv, u_ss.at[2], u_rs.at[2], ctx=1 - c)
    sq.start()
    weight_copies[3].wait()
    weight_copies[4].wait()
    ffe = wg.shape[1]
    hf = ffe // 2

    def gu_copy(f):
        return remote(gusend.at[f], gurecv.at[f], u_ss.at[f], u_rs.at[f], ctx=1 - c)

    own = []
    for f in range(2):
        cut = slice(f * hf, (f + 1) * hf)
        gate, up = mm(xsel[...], wg[:, cut]), mm(xsel[...], wu[:, cut])
        own.append((gate, up))
        gusend[f, 0:slots_n] = gate.astype(BF16)
        gusend[f, slots_n : 2 * slots_n] = up.astype(BF16)
        gu_copy(f).start()
    sq.wait_recv()
    inverse = lax.rsqrt((sumsq + sqrecv[:, 0:1]) / D + epsilon)
    active = []
    for f in range(2):
        gu_copy(f).wait_recv()
        gate = inverse * (own[f][0] + gurecv[f, 0:slots_n].astype(F32))
        up = inverse * (own[f][1] + gurecv[f, slots_n : 2 * slots_n].astype(F32))
        active.append((gate / (1.0 + jnp.exp(-gate)) * up).astype(BF16))
    active = jnp.concatenate(active, axis=1)
    weight_copies[5].wait()
    shape = (devs * 16, 8 * slots_n)
    i, j = iota(shape, 0), iota(shape, 1)
    spread = onehot(j == (((i & 15) >> 1) * slots_n + (i >> 4) * 2 + (i & 1)))

    def back_copy(q, d, back=False):
        to = lax.rem(g + d, devs)
        return remote(
            psend.at[q, to], precv.at[q, to if back else g], p_ss.at[q, to], p_rs.at[q, to if back else g],
            row=to // n_exp, exp=lax.rem(to, n_exp),
        )

    parts = ((0, 8), (8, width // 256))
    for q, (low, high) in enumerate(parts):
        for k in range(low, high):
            row = (k - low) * slots_n
            made[row : row + slots_n, :] = mm(active, wd[:, k * 256 : (k + 1) * 256]).astype(BF16)
        used_rows = (high - low) * slots_n
        sent = mm(spread[:, 0:used_rows], made[0:used_rows, :])
        psend[q] = sent.astype(BF16).reshape(devs, 16, 256)
        precv[q, g] = psend[q, g]
        each(1, devs, lambda d: back_copy(q, d).start())

    shape = (32, devs * 16)
    line, col = iota(shape, 0), iota(shape, 1)
    weights, slots = routing(col >> 4, ids, gates, rows, picks)
    comb = jnp.zeros(shape, F32)
    for b in range(rows):
        here = ((line & 3) == b) & ((line >> 2) == ((col & 15) >> 1)) & ((col & 1) == slots[b])
        comb = jnp.where(here, weights[b], comb)
    high = comb.astype(BF16)
    combine[0:32, :] = high
    combine[32:64, :] = (comb - high.astype(F32)).astype(BF16)

    each(1, devs, lambda d: tile_copy(d).wait_send())
    each(0, rows, lambda b: swap(b).wait_send())
    for b in range(rows):
        each(1, n_exp, lambda d: att_copy(b, d).wait_send())
    for q in range(2):
        term_copy(q).wait_send()
        each(1, n_exp, lambda d: red_copy(q, d).wait_send())
    each(0, 15, lambda i: pass_on(g, i, row=1 - r).wait_send())
    sq.wait_send()
    for f in range(2):
        gu_copy(f).wait_send()

    for q, (low, high) in enumerate(parts):
        each(1, devs, lambda d: back_copy(q, d, True).wait_recv())
        mix = mm(combine[...], precv[q].reshape(devs * 16, 256))
        mix = mix[0:32] + mix[32:64]
        for k in range(low, high):
            cut = slice(k * 256, (k + 1) * 256)
            out[:, cut] = (hid4[:, cut] + mix[4 * (k - low) : 4 * (k - low) + 4]).astype(BF16)
    for q in range(2):
        each(1, devs, lambda d: back_copy(q, d).wait_send())


def fused(
    queries, latent_cache, lengths, w_value, w_out, stream, norm_gain, expert_ids, gate_weights,
    w_gate, w_up, w_down,
):
    rows, heads, qk = queries.shape
    block = latent_cache.shape[1]
    per_dev, latent, v_head = w_value.shape
    width = stream.shape[1]
    n_exp = lax.axis_size("exp")
    devs = n_exp * lax.axis_size("row")
    depth, ffe = w_out.shape[0], w_gate.shape[2]
    part, n_rows, slots_n = width // 4, n_exp * rows, 2 * devs
    vmem, smem, anyw = (pl.BlockSpec(memory_space=s) for s in (pltpu.VMEM, pltpu.SMEM, pl.ANY))
    dma = pltpu.SemaphoreType.DMA
    scratch = [
        pltpu.VMEM((2, qk, block), BF16),
        pltpu.VMEM(w_value.shape, BF16),
        pltpu.VMEM((2, depth, width), BF16),
        pltpu.VMEM((width, ffe), BF16),
        pltpu.VMEM((width, ffe), BF16),
        pltpu.VMEM((ffe, width), BF16),
        pltpu.VMEM((heads, block), F32),
        pltpu.VMEM((rows, 2, heads // 2, latent + 128), BF16),
        pltpu.VMEM((rows, heads // 2, latent + 128), BF16),
        pltpu.VMEM((rows, n_exp, 16, latent // 2), BF16),
        pltpu.VMEM((n_exp, rows, 16, latent // 2), BF16),
        pltpu.VMEM((n_rows, depth), BF16),
        *(
            buffer
            for piece in (512, part - 512)
            for buffer in (
                pltpu.VMEM((4, n_rows, piece), BF16),
                pltpu.VMEM((4, n_rows, piece), F32),
                pltpu.VMEM((4, n_rows, piece), BF16),
                pltpu.VMEM((n_exp, 16, piece), BF16),
                pltpu.VMEM((n_exp, 16, piece), BF16),
            )
        ),
        pltpu.VMEM((rows, width), F32),
        pltpu.VMEM((devs, 16, part), BF16),
        pltpu.VMEM((devs, 8, 128), F32),
        pltpu.VMEM((devs, 8, 128), F32),
        pltpu.VMEM((slots_n, width), BF16),
        pltpu.VMEM((2, 2 * slots_n, ffe // 2), BF16),
        pltpu.VMEM((2, 2 * slots_n, ffe // 2), BF16),
        pltpu.VMEM((slots_n, 128), F32),
        pltpu.VMEM((slots_n, 128), F32),
        pltpu.VMEM((8 * slots_n, 256), BF16),
        pltpu.VMEM((2, devs, 16, 256), BF16),
        pltpu.VMEM((2, devs, 16, 256), BF16),
        pltpu.VMEM((64, devs * 16), BF16),
    ] + [
        dma(s)
        for s in (
            (2, 4), (6, 4), (rows,), (rows,), (rows, n_exp), (rows, n_exp), (2,), (2,), (2, n_exp), (2, n_exp),
            (16,), (devs,), (devs,), (devs,), (3,), (3,), (2, devs), (2, devs),
        )
    ]
    return pl.pallas_call(
        layer_kernel,
        out_shape=jax.ShapeDtypeStruct((rows, width), BF16),
        in_specs=[vmem, anyw, smem, anyw, anyw, vmem, vmem, smem, smem, anyw, anyw, anyw],
        out_specs=vmem,
        scratch_shapes=scratch,
        compiler_params=pltpu.CompilerParams(
            collective_id=0, has_side_effects=True, vmem_limit_bytes=60 * 1024 * 1024
        ),
    )(
        jnp.swapaxes(queries, 1, 2), jnp.swapaxes(latent_cache, 1, 2), lengths, w_value, w_out, stream,
        norm_gain, expert_ids, gate_weights, w_gate, w_up, w_down,
    )


def solution(mesh):
    placed = (
        P(("row", "exp"), None, None),
        P(("row", "exp"), "ctx", None),
        P(("row", "exp")),
        P(("ctx", "exp"), None, None),
        P(("ctx", "exp"), None),
        P(("row", "exp"), "ctx"),
        P("ctx"),
        P(("row", "exp"), None),
        P(("row", "exp"), None),
        P(("row", "exp"), "ctx", None),
        P(("row", "exp"), "ctx", None),
        P(("row", "exp"), None, "ctx"),
    )
    sizes = tuple(mesh.shape[axis] for axis in ("ctx", "row", "exp"))
    body = fused if sizes == (2, 2, 8) else on_device
    return jax.shard_map(
        body, mesh=mesh, in_specs=placed, out_specs=P(("row", "exp"), "ctx"), check_vma=False
    )
```
